256 devices in a mesh: rep: 16 (over z, y_hi), tp: 16 (over y_lo, x, core).
Axes of the slice: x: 4, y: 4 (y_hi: 2, y_lo: 2; y = y_hi * 2 + y_lo), z: 8, core: 2. Of those that a mesh axis runs over, the one named last changes fastest.
Arguments:
- weights: bfloat16 [14336, 4096], P('tp'), may hold values from -0.046875 to 0.046875
- hidden_pool: bfloat16 [16, 512, 14336], P('rep', None, 'tp'), may hold values from -6 to 6
- target_pool: bfloat16 [16, 512, 4096], P('rep', None, 'tp'), may hold values from -6 to 6
- token_rows: int32 [16, 2, 256], P('rep'), may hold values from 0 to 511
- fragment: int32 [1], replicated, may hold values from 0 to 15
- outer_momentum: float32 [14336, 256], P('tp'), may hold values from -0.005859375 to 0.005859375
Outputs:
- new_momentum: float32 [14336, 256], P('tp')
- new_global: float32 [14336, 256], P('tp')
- local_fragment: bfloat16 [16, 14336, 256], P('rep', 'tp')
- last_residual: float32 [16, 4096, 256], P('rep', 'tp')
The draws below stay inside these ranges and needn't reach their ends.
All inputs are finite; a program needn't handle non-finite values.
Results may differ from the reference program's by a relative error of at most 0.033.
Values may be sent and summed in bfloat16 or wider, within the bound.
A program may use at most 192 MiB of HBM per device.

```python
import jax
import jax.numpy as jnp
from jax import lax

D = 4096
FF = 14336
TOK = 256
STEPS = 2
FRAGS = 16
FW = 256
POOL = 512
REPS = 16
N_TP = 16


def touch_ends(entries, stream_key, low, largest):
    longest = entries.shape.index(max(entries.shape))
    spots = []
    for shift in (0, 1):
        where = [jax.random.randint(jax.random.fold_in(stream_key, axis), (), 0, length) for axis, length in enumerate(entries.shape)]
        where[longest] = (where[longest] + shift) % entries.shape[longest]
        spots.append(tuple(where))
    return entries.at[spots[0]].set(low).at[spots[1]].set(largest)


def level_of(key, shape, pieces, smallest, high):
    factor_of = 1.0
    for axis_at, parts in pieces:
        draws = jax.random.uniform(jax.random.fold_in(jax.random.fold_in(key, 6), axis_at), (parts,), jnp.float32, smallest / len(pieces), high / len(pieces))
        factor_of = factor_of * jnp.repeat(jnp.exp(draws), shape[axis_at] // parts).reshape((-1,) + (1,) * (len(shape) - 1 - axis_at))
    return factor_of


def noise(rng, extent, scale, reach, shards=(), kind=jnp.bfloat16):
    values = scale * jax.random.normal(rng, extent, jnp.float32)
    if shards:
        values = values * level_of(rng, extent, shards, -0.22, 0.18)
    return jnp.clip(values, -reach, reach).astype(kind)


def setup_inputs(seed: int = 0) -> dict:
    splits = jax.random.split(jax.random.key(seed), 7)
    return {
        "weights": noise(splits[0], (FF, D), FF ** -0.5, 0.046875, ((0, 16),)),
        "hidden_pool": noise(splits[1], (REPS, POOL, FF), 1.0, 6.0, ((0, 16), (2, 16))),
        "target_pool": noise(splits[2], (REPS, POOL, D), 1.0, 6.0, ((0, 16), (2, 16))),
        "token_rows": touch_ends(jax.random.randint(splits[3], (REPS, STEPS, TOK), 0, POOL), jax.random.fold_in(splits[3], 1), 0, POOL - 1).astype(jnp.int32),
        "fragment": jax.random.randint(splits[4], (1,), 0, FRAGS).astype(jnp.int32),
        "outer_momentum": noise(splits[5], (FF, FW), 0.001, 0.005859375, ((0, 16),), jnp.float32),
    }


BETA_ONE = 0.9
BETA_TWO = 0.95
INNER_RATE = 0.001
DECAY_RATE = 0.1
ADAM_EPS = 0.001
OUTER_RATE = 0.7
OUTER_MOMENTUM = 0.9
MIX_KEEP = 0.5

def forward_sum(hidden, current):
    shard = FF // N_TP

    def add_shard(index, total):
        start = (index * shard).astype(jnp.int32)
        hidden_part = lax.dynamic_slice_in_dim(hidden, start, shard, 1)
        weight_part = lax.dynamic_slice_in_dim(current, start, shard, 0)
        term = jnp.dot(hidden_part, weight_part, preferred_element_type=jnp.float32)
        rounded = lax.optimization_barrier(term.astype(jnp.bfloat16))
        return total + rounded.astype(jnp.float32)
    empty = jnp.zeros((hidden.shape[0], current.shape[1]), jnp.float32)
    return lax.fori_loop(0, N_TP, add_shard, empty)

def adam_update(master, first, second, grad, count):
    first = BETA_ONE * first + (1.0 - BETA_ONE) * grad
    second = BETA_TWO * second + (1.0 - BETA_TWO) * grad * grad
    ratio = first / (1.0 - BETA_ONE ** count) / (jnp.sqrt(second / (1.0 - BETA_TWO ** count)) + ADAM_EPS)
    master = master - INNER_RATE * (ratio + DECAY_RATE * master)
    return (master, first, second)

def reference(weights, hidden_pool, target_pool, token_rows, fragment, outer_momentum):
    width = D // FRAGS
    start = (fragment[0] * width).astype(jnp.int32)
    anchor = lax.dynamic_slice_in_dim(weights, start, width, 1).astype(jnp.float32)

    def replica(items):
        hidden_all, target_all, rows_all = items
        master = weights.astype(jnp.float32)
        first = jnp.zeros_like(master)
        second = jnp.zeros_like(master)
        synced = anchor
        residual_all = jnp.zeros((D, TOK), jnp.float32)
        for step in range(STEPS):
            hidden = jnp.take(hidden_all, rows_all[step], axis=0)
            target = jnp.take(target_all, rows_all[step], axis=0)
            outputs = forward_sum(hidden, master.astype(jnp.bfloat16))
            difference = outputs - target.astype(jnp.float32)
            slope = (difference / TOK).astype(jnp.bfloat16)
            grad = jnp.dot(hidden.T, slope, preferred_element_type=jnp.float32)
            master, first, second = adam_update(master, first, second, grad, step + 1)
            if step == STEPS - 2:
                synced = lax.dynamic_slice_in_dim(master, start, width, 1)
            if step == STEPS - 1:
                residual_all = difference.T
        final = lax.dynamic_slice_in_dim(master, start, width, 1)
        drift = lax.optimization_barrier((anchor - synced).astype(jnp.bfloat16)).astype(jnp.float32)
        return (drift, final, residual_all)
    drifts, finals, residuals = lax.map(replica, (hidden_pool, target_pool, token_rows))
    mean_drift = lax.optimization_barrier(jnp.sum(drifts, axis=0)) / REPS
    new_momentum = OUTER_MOMENTUM * outer_momentum + mean_drift
    new_global = anchor - OUTER_RATE * (mean_drift + OUTER_MOMENTUM * new_momentum)
    local_fragment = (MIX_KEEP * finals + (1.0 - MIX_KEEP) * new_global[None]).astype(jnp.bfloat16)
    return (new_momentum, new_global, local_fragment, residuals)
```

```python
import functools

import jax
import jax.numpy as jnp
from jax import lax
from jax.experimental import pallas as pl
from jax.experimental.pallas import tpu as pltpu
from jax.sharding import PartitionSpec as P

BETA_ONE = 0.9
BETA_TWO = 0.95
INNER_RATE = 0.001
DECAY_RATE = 0.1
ADAM_EPS = 0.001
OUTER_RATE = 0.7
OUTER_MOMENTUM = 0.9
MIX_KEEP = 0.5

MESH = pl.DeviceIdType.MESH
F32 = jnp.float32
BF16 = jnp.bfloat16

NX = 4
NCHIP = 8
NTP = 16
NZ = 8
LANES = 128


def dot(a, b, ca=1, cb=0):
    return lax.dot_general(a, b, (((ca,), (cb,)), ((), ())), preferred_element_type=F32)


def recip(x):
    r = pl.reciprocal(x, approx=True)
    return r * (2.0 - x * r)


def kernel(
    w_hbm, pool_hbm, tpool_hbm, rows_ref, frag_ref, mom_hbm,
    nm_ref, ng_ref, lf_ref, res_ref,
    w_v, pool_v, tpool_v, mom_v,
    h1, h2, ht1, ht2, tgt,
    keep, sibs, sibr, rss, rsr,
    slope0, slope1,
    g1f, synced, drift0, drift1, fpart, frecv, fslope, final,
    zrecv, ysend, yrecv, total,
    w_sem, in_sem,
    sib_s, sib_r, rs_s, rs_r, ag_s, ag_r, agd_s, agd_r,
    f1_s, f1_r, f2_s, f2_r, z1_s, z1_r, y_s, y_r, z2_s, z2_r,
):
    tokens = rows_ref.shape[1]
    pool = pool_v.shape[0]
    depth = w_v.shape[1]
    zrows = depth // NZ
    ftok = tokens // NTP

    me = lax.axis_index("tp")
    core = lax.rem(me, 2)
    chip = lax.div(me, 2)
    cy = lax.div(chip, NX)
    cx = lax.rem(chip, NX)
    rep = lax.axis_index("rep")
    rz = lax.div(rep, 2)
    ry = lax.rem(rep, 2)
    sibling = chip * 2 + 1 - core
    frag = frag_ref[0]
    slopes = (slope0, slope1)
    drifts = (drift0, drift1)

    def chip_at(s):
        return lax.rem(cy + lax.div(s, NX), 2) * NX + lax.rem(cx + lax.rem(s, NX), NX)

    def chip_from(s):
        return lax.rem(cy + lax.div(s, NX), 2) * NX + lax.rem(cx + NX - lax.rem(s, NX), NX)

    def rep_at(s):
        return lax.rem(rz + s, NZ) * 2 + ry

    def loop(lo, hi, body):
        def step(i, carry):
            body(i)
            return carry

        lax.fori_loop(lo, hi, step, 0)

    def w_copy(c, s, j):
        slot = (chip_at(s) * 2 + j) * 2 + c
        return pltpu.make_async_copy(
            w_hbm.at[:, pl.ds(pl.multiple_of(slot * LANES, LANES), LANES)],
            w_v.at[slot],
            w_sem.at[c, s, j],
        )

    pool_copy = pltpu.make_async_copy(pool_hbm.at[0], pool_v, in_sem.at[0])
    tpool_copy = pltpu.make_async_copy(tpool_hbm.at[0], tpool_v, in_sem.at[1])
    mom_copy = pltpu.make_async_copy(mom_hbm, mom_v, in_sem.at[2])
    pool_copy.start()
    for c in range(2):

        def start_w(s, c=c):
            w_copy(c, s, 0).start()
            w_copy(c, s, 1).start()

        loop(0, NCHIP, start_w)
    tpool_copy.start()
    mom_copy.start()

    barrier = pltpu.get_barrier_semaphore()

    def greet_tp(i):
        pl.semaphore_signal(
            barrier, inc=1, device_id={"tp": lax.rem(me + i, NTP)}, device_id_type=MESH
        )

    def greet_z(i):
        pl.semaphore_signal(barrier, inc=1, device_id={"rep": rep_at(i)}, device_id_type=MESH)

    loop(1, NTP, greet_tp)
    loop(1, NZ, greet_z)
    pl.semaphore_signal(barrier, inc=1, device_id={"rep": rz * 2 + 1 - ry}, device_id_type=MESH)

    def picks(k):
        at = lax.broadcasted_iota(jnp.int32, (pool, tokens), 0)
        return jnp.where(at == rows_ref[pl.ds(k, 1), :], 1.0, 0.0).astype(BF16)

    pool_copy.wait()
    h1[...] = dot(picks(0), pool_v[...], 0, 0).astype(BF16)

    pl.semaphore_wait(barrier, NTP - 1 + NZ)

    def sib_copy(u, s):
        return pltpu.make_async_remote_copy(
            src_ref=sibs.at[u, s], dst_ref=sibr.at[u, s],
            send_sem=sib_s.at[u, s], recv_sem=sib_r.at[u, s],
            device_id={"tp": sibling}, device_id_type=MESH,
        )

    def rs_copy(u, s):
        return pltpu.make_async_remote_copy(
            src_ref=rss.at[u, s], dst_ref=rsr.at[u, s],
            send_sem=rs_s.at[u, s], recv_sem=rs_r.at[u, s],
            device_id={"tp": chip_at(s) * 2 + core}, device_id_type=MESH,
        )

    def ag_copy(c, s):
        return pltpu.make_async_remote_copy(
            src_ref=slopes[c].at[me], dst_ref=slopes[c].at[me],
            send_sem=ag_s.at[c, s], recv_sem=ag_r.at[c, s],
            device_id={"tp": chip_at(s) * 2 + core}, device_id_type=MESH,
        )

    def agd_copy(c, s):
        owner = chip_from(s) * 2 + core
        return pltpu.make_async_remote_copy(
            src_ref=slopes[c].at[owner], dst_ref=slopes[c].at[owner],
            send_sem=agd_s.at[c, s], recv_sem=agd_r.at[c, s],
            device_id={"tp": sibling}, device_id_type=MESH,
        )

    def ftoks(i):
        return pl.ds(pl.multiple_of(i * ftok, ftok), ftok)

    def f1_copy(i):
        to = lax.rem(me + i, NTP)
        return pltpu.make_async_remote_copy(
            src_ref=fpart.at[:, ftoks(to), :], dst_ref=frecv.at[i],
            send_sem=f1_s.at[i], recv_sem=f1_r.at[i],
            device_id={"tp": to}, device_id_type=MESH,
        )

    def f2_copy(i):
        to = lax.rem(me + i, NTP)
        return pltpu.make_async_remote_copy(
            src_ref=fslope.at[:, ftoks(me), :], dst_ref=fslope.at[:, ftoks(me), :],
            send_sem=f2_s.at[i], recv_sem=f2_r.at[i],
            device_id={"tp": to}, device_id_type=MESH,
        )

    def zpart(i):
        return pl.ds(pl.multiple_of(i * zrows, 16), zrows)

    def z1_copy(c, s):
        return pltpu.make_async_remote_copy(
            src_ref=drifts[c].at[zpart(lax.rem(rz + s, NZ)), :], dst_ref=zrecv.at[c, s],
            send_sem=z1_s.at[c, s], recv_sem=z1_r.at[c, s],
            device_id={"rep": rep_at(s)}, device_id_type=MESH,
        )

    def y_copy(c):
        return pltpu.make_async_remote_copy(
            src_ref=ysend.at[c], dst_ref=yrecv.at[c],
            send_sem=y_s.at[c], recv_sem=y_r.at[c],
            device_id={"rep": rz * 2 + 1 - ry}, device_id_type=MESH,
        )

    def z2_copy(c, s):
        return pltpu.make_async_remote_copy(
            src_ref=total.at[c, zpart(rz), :], dst_ref=total.at[c, zpart(rz), :],
            send_sem=z2_s.at[c, s], recv_sem=z2_r.at[c, s],
            device_id={"rep": rep_at(s)}, device_id_type=MESH,
        )

    def w_pair(c, s):
        q = chip_at(s)
        mine = w_v[(q * 2 + core) * 2 + c]
        other = w_v[(q * 2 + 1 - core) * 2 + c]
        return jnp.concatenate([mine, other], axis=1)

    def part_out(u, s, part):
        keep[u, s] = part[:, :LANES].astype(BF16)
        sibs[u, s] = part[:, LANES:].astype(BF16)
        sib_copy(u, s).start()

    def forward_one(c):
        def body(s):
            w_copy(c, s, 0).wait()
            w_copy(c, s, 1).wait()
            part_out(c, s, dot(h1[...], w_pair(c, s)))

        loop(0, NCHIP, body)

    def reduce_send(u):
        def body(s):
            sib_copy(u, s).wait_recv()
            rss[u, s] = (keep[u, s].astype(F32) + sibr[u, s].astype(F32)).astype(BF16)
            rs_copy(u, s).start()

        loop(1, NCHIP, body)

    def own_sum(u):
        sib_copy(u, 0).wait_recv()
        acc = keep[u, 0].astype(F32) + sibr[u, 0].astype(F32)
        for s in range(1, NCHIP):
            rs_copy(u, s).wait_recv()
            acc = acc + rsr[u, s].astype(F32)
        return acc

    def lanes(c):
        return pl.ds(c * LANES, LANES)

    def slope_send(c):
        diff = own_sum(c) - tgt[0, :, lanes(c)].astype(F32)
        slopes[c][me] = (diff * (1.0 / tokens)).astype(BF16)
        agd_copy(c, 0).start()
        loop(1, NCHIP, lambda s: ag_copy(c, s).start())

    def step_one_columns(c):
        slope = slopes[c]

        def body(s):
            q = chip_from(s)

            @pl.when(s > 0)
            def _():
                ag_copy(c, s).wait_recv()
                agd_copy(c, s).start()

            agd_copy(c, s).wait_recv()
            pair = jnp.concatenate([slope[q * 2 + core], slope[q * 2 + 1 - core]], axis=1)
            grad = dot(ht1[...], pair)
            mine = w_v[(q * 2 + core) * 2 + c]
            other = w_v[(q * 2 + 1 - core) * 2 + c]
            w = jnp.concatenate([mine, other], axis=1).astype(F32)
            ratio = grad * recip(jnp.abs(grad) + ADAM_EPS)
            cur = (w - INNER_RATE * (ratio + DECAY_RATE * w)).astype(BF16)
            t = lax.div(s, NX) * NX + lax.rem(NX - lax.rem(s, NX), NX)
            part_out(2 + c, t, dot(h2[...], cur))

        loop(0, NCHIP, body)

    def fragment_one(c):
        grad = dot(ht1[...], slopes[c][frag])
        anchor = w_v[frag * 2 + c].astype(F32)
        ratio = grad * recip(jnp.abs(grad) + ADAM_EPS)
        after = anchor - INNER_RATE * (ratio + DECAY_RATE * anchor)
        g1f[c] = grad
        synced[c] = after
        drifts[c][...] = (anchor - after).astype(BF16)
        loop(1, NZ, lambda s: z1_copy(c, s).start())
        part = dot(h2[...], after.astype(BF16))
        taken = jnp.where(frag == me, 1.0, 0.0) * tgt[1, :, lanes(c)].astype(F32)
        fpart[c] = (part - taken).astype(BF16)

    def z_sum(c):
        acc = drifts[c][zpart(rz), :].astype(F32)
        for s in range(1, NZ):
            z1_copy(c, s).wait_recv()
            acc = acc + zrecv[c, s].astype(F32)
        ysend[c] = acc.astype(BF16)
        y_copy(c).start()

    def y_sum(c):
        y_copy(c).wait_recv()
        total[c, zpart(rz), :] = (ysend[c].astype(F32) + yrecv[c].astype(F32)).astype(BF16)
        loop(1, NZ, lambda s: z2_copy(c, s).start())

    def fragment_slope():
        acc = fpart[:, ftoks(me), :].astype(F32)
        for i in range(1, NTP):
            f1_copy(i).wait_recv()
            acc = acc + frecv[i].astype(F32)
        fslope[:, ftoks(me), :] = (acc * (1.0 / tokens)).astype(BF16)
        loop(1, NTP, lambda i: f2_copy(i).start())

    def fragment_two():
        loop(1, NTP, lambda i: f2_copy(i).wait_recv())
        for c in range(2):
            grad = dot(ht2[...], fslope[c])
            one = g1f[c]
            first = BETA_ONE * (1.0 - BETA_ONE) * one + (1.0 - BETA_ONE) * grad
            second = BETA_TWO * (1.0 - BETA_TWO) * one * one + (1.0 - BETA_TWO) * grad * grad
            ratio = (first * (1.0 / (1.0 - BETA_ONE**2))) / (
                jnp.sqrt(second * (1.0 / (1.0 - BETA_TWO**2))) + ADAM_EPS
            )
            after = synced[c]
            final[c] = after - INNER_RATE * (ratio + DECAY_RATE * after)

    def residual_out(c):
        diff = own_sum(2 + c) - tgt[1, :, lanes(c)].astype(F32)
        res_ref[0, lanes(c), :] = diff.T

    def outer(c):
        loop(1, NZ, lambda s: z2_copy(c, s).wait_recv())
        anchor = w_v[frag * 2 + c].astype(F32)
        mean = total[c].astype(F32) * (1.0 / (2 * NZ))
        moved = OUTER_MOMENTUM * mom_v[:, lanes(c)] + mean
        new = anchor - OUTER_RATE * (mean + OUTER_MOMENTUM * moved)
        nm_ref[:, lanes(c)] = moved
        ng_ref[:, lanes(c)] = new
        lf_ref[0, :, lanes(c)] = (MIX_KEEP * final[c] + (1.0 - MIX_KEEP) * new).astype(BF16)

    forward_one(0)
    reduce_send(0)
    forward_one(1)
    reduce_send(1)
    ht1[...] = dot(pool_v[...], picks(0), 0, 0).astype(BF16)
    h2[...] = dot(picks(1), pool_v[...], 0, 0).astype(BF16)
    tpool_copy.wait()
    for k in range(2):
        tgt[k] = dot(picks(k), tpool_v[...], 0, 0).astype(BF16)
    slope_send(0)
    ht2[...] = dot(pool_v[...], picks(1), 0, 0).astype(BF16)
    slope_send(1)
    step_one_columns(0)
    reduce_send(2)
    fragment_one(0)
    step_one_columns(1)
    reduce_send(3)
    fragment_one(1)
    loop(1, NTP, lambda i: f1_copy(i).start())
    z_sum(0)
    fragment_slope()
    y_sum(0)
    residual_out(0)
    z_sum(1)
    fragment_two()
    y_sum(1)
    mom_copy.wait()
    outer(0)
    residual_out(1)
    outer(1)

    for u in range(4):
        loop(0, NCHIP, lambda s, u=u: sib_copy(u, s).wait_send())
        loop(1, NCHIP, lambda s, u=u: rs_copy(u, s).wait_send())
    for c in range(2):
        loop(1, NCHIP, lambda s, c=c: ag_copy(c, s).wait_send())
        loop(0, NCHIP, lambda s, c=c: agd_copy(c, s).wait_send())
        loop(1, NZ, lambda s, c=c: z1_copy(c, s).wait_send())
        y_copy(c).wait_send()
        loop(1, NZ, lambda s, c=c: z2_copy(c, s).wait_send())
    loop(1, NTP, lambda i: f1_copy(i).wait_send())
    loop(1, NTP, lambda i: f2_copy(i).wait_send())


def body(weights, hidden_pool, target_pool, token_rows, fragment, outer_momentum):
    depth, features = weights.shape
    pool = hidden_pool.shape[1]
    width = outer_momentum.shape[1]
    owned = target_pool.shape[2]
    tokens = token_rows.shape[2]
    zrows = depth // NZ
    blocks = features // LANES
    dma = pltpu.SemaphoreType.DMA
    scratch = [
        pltpu.VMEM((blocks, depth, LANES), BF16),
        pltpu.VMEM((pool, depth), BF16),
        pltpu.VMEM((pool, owned), BF16),
        pltpu.VMEM((depth, width), F32),
        pltpu.VMEM((tokens, depth), BF16),
        pltpu.VMEM((tokens, depth), BF16),
        pltpu.VMEM((depth, tokens), BF16),
        pltpu.VMEM((depth, tokens), BF16),
        pltpu.VMEM((2, tokens, owned), BF16),
        *[pltpu.VMEM((4, NCHIP, tokens, LANES), BF16)] * 5,
        *[pltpu.VMEM((NTP, tokens, LANES), BF16)] * 2,
        pltpu.VMEM((2, depth, LANES), F32),
        pltpu.VMEM((2, depth, LANES), F32),
        *[pltpu.VMEM((depth, LANES), BF16)] * 2,
        pltpu.VMEM((2, tokens, LANES), BF16),
        pltpu.VMEM((NTP, 2, tokens // NTP, LANES), BF16),
        pltpu.VMEM((2, tokens, LANES), BF16),
        pltpu.VMEM((2, depth, LANES), F32),
        pltpu.VMEM((2, NZ, zrows, LANES), BF16),
        pltpu.VMEM((2, zrows, LANES), BF16),
        pltpu.VMEM((2, zrows, LANES), BF16),
        pltpu.VMEM((2, depth, LANES), BF16),
        dma((2, NCHIP, 2)),
        dma((3,)),
        *[dma((4, NCHIP))] * 4,
        *[dma((2, NCHIP))] * 4,
        *[dma((NTP,))] * 4,
        dma((2, NZ)),
        dma((2, NZ)),
        dma((2,)),
        dma((2,)),
        dma((2, NZ)),
        dma((2, NZ)),
    ]
    hbm = pl.BlockSpec(memory_space=pl.ANY)
    vmem = pl.BlockSpec(memory_space=pltpu.VMEM)
    smem = pl.BlockSpec(memory_space=pltpu.SMEM)
    return pl.pallas_call(
        kernel,
        out_shape=(
            jax.ShapeDtypeStruct((depth, width), F32),
            jax.ShapeDtypeStruct((depth, width), F32),
            jax.ShapeDtypeStruct((1, depth, width), BF16),
            jax.ShapeDtypeStruct((1, owned, tokens), F32),
        ),
        in_specs=[hbm, hbm, hbm, vmem, smem, hbm],
        out_specs=(vmem, vmem, vmem, vmem),
        scratch_shapes=scratch,
        compiler_params=pltpu.CompilerParams(
            collective_id=0, has_side_effects=True, vmem_limit_bytes=56 * 1024 * 1024
        ),
    )(weights, hidden_pool, target_pool, token_rows[0], fragment, outer_momentum)


def solution(mesh):
    in_specs = (
        P("tp", None),
        P("rep", None, "tp"),
        P("rep", None, "tp"),
        P("rep", None, None),
        P(),
        P("tp", None),
    )
    out_specs = (P("tp", None), P("tp", None), P("rep", "tp", None), P("rep", "tp", None))
    return jax.shard_map(body, mesh=mesh, in_specs=in_specs, out_specs=out_specs, check_vma=False)
```

```python
import functools

import jax
import jax.numpy as jnp
from jax import lax
from jax.experimental import pallas as pl
from jax.experimental.pallas import tpu as pltpu
from jax.sharding import PartitionSpec as P

BETA_ONE = 0.9
BETA_TWO = 0.95
INNER_RATE = 0.001
DECAY_RATE = 0.1
ADAM_EPS = 0.001
OUTER_RATE = 0.7
OUTER_MOMENTUM = 0.9
MIX_KEEP = 0.5

MESH = pl.DeviceIdType.MESH
F32 = jnp.float32
BF16 = jnp.bfloat16

NX = 4
NCHIP = 8
NTP = 16
NZ = 8
LANES = 128


def dot(a, b, ca=1, cb=0):
    return lax.dot_general(a, b, (((ca,), (cb,)), ((), ())), preferred_element_type=F32)


def recip(x):
    r = pl.reciprocal(x, approx=True)
    return r * (2.0 - x * r)


def kernel(
    w_hbm, pool_hbm, tpool_hbm, rows_ref, frag_ref, mom_hbm,
    nm_ref, ng_ref, lf_ref, res_ref,
    w_v, pool_v, tpool_v, mom_v,
    h1, h2, ht1, ht2, tgt,
    keep, sibs, sibr, rss, rsr,
    slope0, slope1, grad0, grad1, cur0, cur1,
    g1f, synced, drift0, drift1, fpart, frecv, fslope, final,
    zrecv, ysend, yrecv, total,
    w_sem, in_sem,
    sib_s, sib_r, rs_s, rs_r, ag_s, ag_r, agd_s, agd_r,
    f1_s, f1_r, f2_s, f2_r, z1_s, z1_r, y_s, y_r, z2_s, z2_r,
):
    tokens = rows_ref.shape[1]
    pool = pool_v.shape[0]
    depth = w_v.shape[1]
    zrows = depth // NZ
    ftok = tokens // NTP

    me = lax.axis_index("tp")
    core = lax.rem(me, 2)
    chip = lax.div(me, 2)
    cy = lax.div(chip, NX)
    cx = lax.rem(chip, NX)
    rep = lax.axis_index("rep")
    rz = lax.div(rep, 2)
    ry = lax.rem(rep, 2)
    sibling = chip * 2 + 1 - core
    frag = frag_ref[0]
    slopes = (slope0, slope1)
    drifts = (drift0, drift1)
    grads = (grad0, grad1)
    currents = (cur0, cur1)

    def chip_at(s):
        return lax.rem(cy + lax.div(s, NX), 2) * NX + lax.rem(cx + lax.rem(s, NX), NX)

    def chip_from(s):
        return lax.rem(cy + lax.div(s, NX), 2) * NX + lax.rem(cx + NX - lax.rem(s, NX), NX)

    def slot_of(s):
        return s // NX * NX + (NX - s % NX) % NX

    def rep_at(s):
        return lax.rem(rz + s, NZ) * 2 + ry

    def loop(lo, hi, body):
        def step(i, carry):
            body(i)
            return carry

        lax.fori_loop(lo, hi, step, 0)

    def w_copy(c, s, j):
        slot = (chip_at(s) * 2 + j) * 2 + c
        return pltpu.make_async_copy(
            w_hbm.at[:, pl.ds(pl.multiple_of(slot * LANES, LANES), LANES)],
            w_v.at[slot],
            w_sem.at[c, s, j],
        )

    pool_copy = pltpu.make_async_copy(pool_hbm.at[0], pool_v, in_sem.at[0])
    tpool_copy = pltpu.make_async_copy(tpool_hbm.at[0], tpool_v, in_sem.at[1])
    mom_copy = pltpu.make_async_copy(mom_hbm, mom_v, in_sem.at[2])
    pool_copy.start()
    for c in range(2):

        def start_w(s, c=c):
            w_copy(c, s, 0).start()
            w_copy(c, s, 1).start()

        loop(0, NCHIP, start_w)
    tpool_copy.start()
    mom_copy.start()

    barrier = pltpu.get_barrier_semaphore()

    def greet_tp(i):
        pl.semaphore_signal(
            barrier, inc=1, device_id={"tp": lax.rem(me + i, NTP)}, device_id_type=MESH
        )

    def greet_z(i):
        pl.semaphore_signal(barrier, inc=1, device_id={"rep": rep_at(i)}, device_id_type=MESH)

    loop(1, NTP, greet_tp)
    loop(1, NZ, greet_z)
    pl.semaphore_signal(barrier, inc=1, device_id={"rep": rz * 2 + 1 - ry}, device_id_type=MESH)

    def picks(k):
        at = lax.broadcasted_iota(jnp.int32, (pool, tokens), 0)
        return jnp.where(at == rows_ref[pl.ds(k, 1), :], 1.0, 0.0).astype(BF16)

    pool_copy.wait()
    h1[...] = dot(picks(0), pool_v[...], 0, 0).astype(BF16)

    pl.semaphore_wait(barrier, NTP - 1 + NZ)

    def sib_copy(u, s):
        return pltpu.make_async_remote_copy(
            src_ref=sibs.at[u, s], dst_ref=sibr.at[u, s],
            send_sem=sib_s.at[u, s], recv_sem=sib_r.at[u, s],
            device_id={"tp": sibling}, device_id_type=MESH,
        )

    def rs_copy(u, s):
        return pltpu.make_async_remote_copy(
            src_ref=rss.at[u, s], dst_ref=rsr.at[u, s],
            send_sem=rs_s.at[u, s], recv_sem=rs_r.at[u, s],
            device_id={"tp": chip_at(s) * 2 + core}, device_id_type=MESH,
        )

    def ag_copy(c, s):
        return pltpu.make_async_remote_copy(
            src_ref=slopes[c].at[me], dst_ref=slopes[c].at[me],
            send_sem=ag_s.at[c, s], recv_sem=ag_r.at[c, s],
            device_id={"tp": chip_at(s) * 2 + core}, device_id_type=MESH,
        )

    def agd_copy(c, s):
        owner = chip_from(s) * 2 + core
        return pltpu.make_async_remote_copy(
            src_ref=slopes[c].at[owner], dst_ref=slopes[c].at[owner],
            send_sem=agd_s.at[c, s], recv_sem=agd_r.at[c, s],
            device_id={"tp": sibling}, device_id_type=MESH,
        )

    def ftoks(i):
        return pl.ds(pl.multiple_of(i * ftok, ftok), ftok)

    def f1_copy(i):
        to = lax.rem(me + i, NTP)
        return pltpu.make_async_remote_copy(
            src_ref=fpart.at[:, ftoks(to), :], dst_ref=frecv.at[i],
            send_sem=f1_s.at[i], recv_sem=f1_r.at[i],
            device_id={"tp": to}, device_id_type=MESH,
        )

    def f2_copy(i):
        to = lax.rem(me + i, NTP)
        return pltpu.make_async_remote_copy(
            src_ref=fslope.at[:, ftoks(me), :], dst_ref=fslope.at[:, ftoks(me), :],
            send_sem=f2_s.at[i], recv_sem=f2_r.at[i],
            device_id={"tp": to}, device_id_type=MESH,
        )

    def zpart(i):
        return pl.ds(pl.multiple_of(i * zrows, 16), zrows)

    def z1_copy(c, s):
        return pltpu.make_async_remote_copy(
            src_ref=drifts[c].at[zpart(lax.rem(rz + s, NZ)), :], dst_ref=zrecv.at[c, s],
            send_sem=z1_s.at[c, s], recv_sem=z1_r.at[c, s],
            device_id={"rep": rep_at(s)}, device_id_type=MESH,
        )

    def y_copy(c):
        return pltpu.make_async_remote_copy(
            src_ref=ysend.at[c], dst_ref=yrecv.at[c],
            send_sem=y_s.at[c], recv_sem=y_r.at[c],
            device_id={"rep": rz * 2 + 1 - ry}, device_id_type=MESH,
        )

    def z2_copy(c, s):
        return pltpu.make_async_remote_copy(
            src_ref=total.at[c, zpart(rz), :], dst_ref=total.at[c, zpart(rz), :],
            send_sem=z2_s.at[c, s], recv_sem=z2_r.at[c, s],
            device_id={"rep": rep_at(s)}, device_id_type=MESH,
        )

    def w_pair(c, s):
        q = chip_at(s)
        mine = w_v[(q * 2 + core) * 2 + c]
        other = w_v[(q * 2 + 1 - core) * 2 + c]
        return jnp.concatenate([mine, other], axis=1)

    def forward_one(c):
        for s in range(0, NCHIP, 2):
            for t in (s, s + 1):
                w_copy(c, t, 0).wait()
                w_copy(c, t, 1).wait()
            for t in (s, s + 1):
                part = dot(h1[...], w_pair(c, t))
                keep[c, t] = part[:, :LANES].astype(BF16)
                sibs[c, t] = part[:, LANES:].astype(BF16)
            for t in (s, s + 1):
                sib_copy(c, t).start()

    def reduce_send(u):
        def body(s):
            sib_copy(u, s).wait_recv()
            rss[u, s] = (keep[u, s].astype(F32) + sibr[u, s].astype(F32)).astype(BF16)
            rs_copy(u, s).start()

        loop(1, NCHIP, body)

    def own_sum(u):
        sib_copy(u, 0).wait_recv()
        acc = keep[u, 0].astype(F32) + sibr[u, 0].astype(F32)
        for s in range(1, NCHIP):
            rs_copy(u, s).wait_recv()
            acc = acc + rsr[u, s].astype(F32)
        return acc

    def lanes(c):
        return pl.ds(c * LANES, LANES)

    def slope_send(c):
        diff = own_sum(c) - tgt[0, :, lanes(c)].astype(F32)
        slopes[c][me] = (diff * (1.0 / tokens)).astype(BF16)
        agd_copy(c, 0).start()
        loop(1, NCHIP, lambda s: ag_copy(c, s).start())

    def step_one_columns(c):
        slope = slopes[c]

        def gradient(s):
            q = chip_from(s)
            pair = jnp.concatenate([slope[q * 2 + core], slope[q * 2 + 1 - core]], axis=1)
            grads[s % 2][...] = dot(ht1[...], pair)

        def adamw(s):
            q = chip_from(s)
            mine = w_v[(q * 2 + core) * 2 + c]
            other = w_v[(q * 2 + 1 - core) * 2 + c]
            w = jnp.concatenate([mine, other], axis=1).astype(F32)
            grad = grads[s % 2][...]
            scale = pl.reciprocal(jnp.abs(grad) * (1.0 / INNER_RATE) + ADAM_EPS / INNER_RATE, approx=True)
            currents[s % 2][...] = (w * (1.0 - INNER_RATE * DECAY_RATE) - grad * scale).astype(BF16)

        def forward_two(s):
            t = slot_of(s)
            part = dot(h2[...], currents[s % 2][...])
            keep[2 + c, t] = part[:, :LANES].astype(BF16)
            sibs[2 + c, t] = part[:, LANES:].astype(BF16)

        for i in range(NCHIP + 2):
            if i < NCHIP and c == 0:
                agd_copy(c, i).wait_recv()
            if i >= 2:
                forward_two(i - 2)
            if 1 <= i < NCHIP + 1:
                adamw(i - 1)
            if i < NCHIP:
                gradient(i)
            if i >= 2:
                sib_copy(2 + c, slot_of(i - 2)).start()

    def hand_over(c):
        def body(s):
            ag_copy(c, s).wait_recv()
            agd_copy(c, s).start()

        loop(1, NCHIP, body)

    def fragment_one(c):
        grad = dot(ht1[...], slopes[c][frag])
        anchor = w_v[frag * 2 + c].astype(F32)
        ratio = grad * recip(jnp.abs(grad) + ADAM_EPS)
        after = anchor - INNER_RATE * (ratio + DECAY_RATE * anchor)
        g1f[c] = grad
        synced[c] = after
        drifts[c][...] = (anchor - after).astype(BF16)
        loop(1, NZ, lambda s: z1_copy(c, s).start())
        part = dot(h2[...], after.astype(BF16))
        taken = jnp.where(frag == me, 1.0, 0.0) * tgt[1, :, lanes(c)].astype(F32)
        fpart[c] = (part - taken).astype(BF16)

    def z_sum(c):
        acc = drifts[c][zpart(rz), :].astype(F32)
        for s in range(1, NZ):
            z1_copy(c, s).wait_recv()
            acc = acc + zrecv[c, s].astype(F32)
        ysend[c] = acc.astype(BF16)
        y_copy(c).start()

    def y_sum(c):
        y_copy(c).wait_recv()
        total[c, zpart(rz), :] = (ysend[c].astype(F32) + yrecv[c].astype(F32)).astype(BF16)
        loop(1, NZ, lambda s: z2_copy(c, s).start())

    def fragment_slope():
        acc = fpart[:, ftoks(me), :].astype(F32)
        for i in range(1, NTP):
            f1_copy(i).wait_recv()
            acc = acc + frecv[i].astype(F32)
        fslope[:, ftoks(me), :] = (acc * (1.0 / tokens)).astype(BF16)
        loop(1, NTP, lambda i: f2_copy(i).start())

    def fragment_two():
        loop(1, NTP, lambda i: f2_copy(i).wait_recv())
        for c in range(2):
            grad = dot(ht2[...], fslope[c])
            one = g1f[c]
            first = BETA_ONE * (1.0 - BETA_ONE) * one + (1.0 - BETA_ONE) * grad
            second = BETA_TWO * (1.0 - BETA_TWO) * one * one + (1.0 - BETA_TWO) * grad * grad
            ratio = (first * (1.0 / (1.0 - BETA_ONE**2))) / (
                jnp.sqrt(second * (1.0 / (1.0 - BETA_TWO**2))) + ADAM_EPS
            )
            after = synced[c]
            final[c] = after - INNER_RATE * (ratio + DECAY_RATE * after)

    def residual_out(c):
        diff = own_sum(2 + c) - tgt[1, :, lanes(c)].astype(F32)
        res_ref[0, lanes(c), :] = diff.T

    def outer(c):
        loop(1, NZ, lambda s: z2_copy(c, s).wait_recv())
        anchor = w_v[frag * 2 + c].astype(F32)
        mean = total[c].astype(F32) * (1.0 / (2 * NZ))
        moved = OUTER_MOMENTUM * mom_v[:, lanes(c)] + mean
        new = anchor - OUTER_RATE * (mean + OUTER_MOMENTUM * moved)
        nm_ref[:, lanes(c)] = moved
        ng_ref[:, lanes(c)] = new
        lf_ref[0, :, lanes(c)] = (MIX_KEEP * final[c] + (1.0 - MIX_KEEP) * new).astype(BF16)

    forward_one(0)
    reduce_send(0)
    forward_one(1)
    reduce_send(1)
    ht1[...] = dot(pool_v[...], picks(0), 0, 0).astype(BF16)
    h2[...] = dot(picks(1), pool_v[...], 0, 0).astype(BF16)
    tpool_copy.wait()
    for k in range(2):
        tgt[k] = dot(picks(k), tpool_v[...], 0, 0).astype(BF16)
    slope_send(0)
    ht2[...] = dot(pool_v[...], picks(1), 0, 0).astype(BF16)
    slope_send(1)
    hand_over(0)
    step_one_columns(0)
    reduce_send(2)
    fragment_one(0)
    hand_over(1)
    loop(0, NCHIP, lambda s: agd_copy(1, s).wait_recv())
    fragment_one(1)
    loop(1, NTP, lambda i: f1_copy(i).start())
    step_one_columns(1)
    reduce_send(3)
    z_sum(0)
    fragment_slope()
    z_sum(1)
    y_sum(0)
    y_sum(1)
    fragment_two()
    mom_copy.wait()
    residual_out(0)
    outer(0)
    outer(1)
    residual_out(1)

    for u in range(4):
        loop(0, NCHIP, lambda s, u=u: sib_copy(u, s).wait_send())
        loop(1, NCHIP, lambda s, u=u: rs_copy(u, s).wait_send())
    for c in range(2):
        loop(1, NCHIP, lambda s, c=c: ag_copy(c, s).wait_send())
        loop(0, NCHIP, lambda s, c=c: agd_copy(c, s).wait_send())
        loop(1, NZ, lambda s, c=c: z1_copy(c, s).wait_send())
        y_copy(c).wait_send()
        loop(1, NZ, lambda s, c=c: z2_copy(c, s).wait_send())
    loop(1, NTP, lambda i: f1_copy(i).wait_send())
    loop(1, NTP, lambda i: f2_copy(i).wait_send())


def copy_out(*refs):
    sem = refs[-1]
    copies = [pltpu.make_async_copy(refs[i], refs[4 + i], sem.at[i]) for i in range(4)]
    for copy in copies:
        copy.start()
    for copy in copies:
        copy.wait()


def body(weights, hidden_pool, target_pool, token_rows, fragment, outer_momentum):
    depth, features = weights.shape
    pool = hidden_pool.shape[1]
    width = outer_momentum.shape[1]
    owned = target_pool.shape[2]
    tokens = token_rows.shape[2]
    zrows = depth // NZ
    blocks = features // LANES
    dma = pltpu.SemaphoreType.DMA
    scratch = [
        pltpu.VMEM((blocks, depth, LANES), BF16),
        pltpu.VMEM((pool, depth), BF16),
        pltpu.VMEM((pool, owned), BF16),
        pltpu.VMEM((depth, width), F32),
        pltpu.VMEM((tokens, depth), BF16),
        pltpu.VMEM((tokens, depth), BF16),
        pltpu.VMEM((depth, tokens), BF16),
        pltpu.VMEM((depth, tokens), BF16),
        pltpu.VMEM((2, tokens, owned), BF16),
        *[pltpu.VMEM((4, NCHIP, tokens, LANES), BF16)] * 5,
        *[pltpu.VMEM((NTP, tokens, LANES), BF16)] * 2,
        *[pltpu.VMEM((depth, 2 * LANES), F32)] * 2,
        *[pltpu.VMEM((depth, 2 * LANES), BF16)] * 2,
        pltpu.VMEM((2, depth, LANES), F32),
        pltpu.VMEM((2, depth, LANES), F32),
        *[pltpu.VMEM((depth, LANES), BF16)] * 2,
        pltpu.VMEM((2, tokens, LANES), BF16),
        pltpu.VMEM((NTP, 2, tokens // NTP, LANES), BF16),
        pltpu.VMEM((2, tokens, LANES), BF16),
        pltpu.VMEM((2, depth, LANES), F32),
        pltpu.VMEM((2, NZ, zrows, LANES), BF16),
        pltpu.VMEM((2, zrows, LANES), BF16),
        pltpu.VMEM((2, zrows, LANES), BF16),
        pltpu.VMEM((2, depth, LANES), BF16),
        dma((2, NCHIP, 2)),
        dma((3,)),
        *[dma((4, NCHIP))] * 4,
        *[dma((2, NCHIP))] * 4,
        *[dma((NTP,))] * 4,
        dma((2, NZ)),
        dma((2, NZ)),
        dma((2,)),
        dma((2,)),
        dma((2, NZ)),
        dma((2, NZ)),
    ]
    hbm = pl.BlockSpec(memory_space=pl.ANY)
    vmem = pl.BlockSpec(memory_space=pltpu.VMEM)
    smem = pl.BlockSpec(memory_space=pltpu.SMEM)
    results = (
        jax.ShapeDtypeStruct((depth, width), F32),
        jax.ShapeDtypeStruct((depth, width), F32),
        jax.ShapeDtypeStruct((1, depth, width), BF16),
        jax.ShapeDtypeStruct((1, owned, tokens), F32),
    )
    held = pl.pallas_call(
        kernel,
        out_shape=tuple(pltpu.VMEM(r.shape, r.dtype) for r in results),
        in_specs=[hbm, hbm, hbm, vmem, smem, hbm],
        out_specs=(vmem, vmem, vmem, vmem),
        scratch_shapes=scratch,
        compiler_params=pltpu.CompilerParams(
            collective_id=0, has_side_effects=True, vmem_limit_bytes=56 * 1024 * 1024
        ),
    )(weights, hidden_pool, target_pool, token_rows[0], fragment, outer_momentum)
    return pl.pallas_call(
        copy_out,
        out_shape=results,
        in_specs=[hbm] * 4,
        out_specs=(hbm,) * 4,
        scratch_shapes=[dma((4,))],
        compiler_params=pltpu.CompilerParams(vmem_limit_bytes=4 * 1024 * 1024),
    )(*held)


def solution(mesh):
    in_specs = (
        P("tp", None),
        P("rep", None, "tp"),
        P("rep", None, "tp"),
        P("rep", None, None),
        P(),
        P("tp", None),
    )
    out_specs = (P("tp", None), P("tp", None), P("rep", "tp", None), P("rep", "tp", None))
    return jax.shard_map(body, mesh=mesh, in_specs=in_specs, out_specs=out_specs, check_vma=False)
```

```python
import functools

import jax
import jax.numpy as jnp
from jax import lax
from jax.experimental import pallas as pl
from jax.experimental.pallas import tpu as pltpu
from jax.sharding import PartitionSpec as P

BETA_ONE = 0.9
BETA_TWO = 0.95
INNER_RATE = 0.001
DECAY_RATE = 0.1
ADAM_EPS = 0.001
OUTER_RATE = 0.7
OUTER_MOMENTUM = 0.9
MIX_KEEP = 0.5

MESH = pl.DeviceIdType.MESH
F32 = jnp.float32
BF16 = jnp.bfloat16

NX = 4
NCHIP = 8
NTP = 16
NZ = 8
LANES = 128


def dot(a, b, ca=1, cb=0):
    return lax.dot_general(a, b, (((ca,), (cb,)), ((), ())), preferred_element_type=F32)


def recip(x):
    r = pl.reciprocal(x, approx=True)
    return r * (2.0 - x * r)


AHEAD, BEHIND, ACROSS = 1, NX - 1, NX
HOPS = (
    (6, None, AHEAD),
    (7, None, BEHIND),
    (2, None, BEHIND),
    (5, 0, ACROSS),
    (4, 1, ACROSS),
    (3, 2, BEHIND),
    (1, 3, AHEAD),
)
LAST_HOPS = (4, 5, 6)
SPREAD = (
    (0, AHEAD, 3),
    (0, BEHIND, 1),
    (0, ACROSS, 4),
    (1, ACROSS, 5),
    (4, AHEAD, 7),
    (3, AHEAD, 2),
    (5, BEHIND, 6),
)
OUTWARD = (6, 2, 7, 5, 4, 3, 1, 0)
GROUPS = (
    ((0, 0), (1, 0)),
    ((0, 1), (0, 3)),
    ((0, 4), (1, 1)),
    ((1, 3), (1, 4)),
    ((0, 5), (0, 7)),
    ((0, 2), (1, 5)),
    ((1, 7), (1, 2)),
    ((0, 6), (1, 6)),
)


def mirror(r):
    return r // NX * NX + (NX - r % NX) % NX


def kernel(
    w_hbm, pool_hbm, tpool_hbm, rows_ref, frag_ref, mom_hbm,
    nm_ref, ng_ref, lf_ref, res_ref,
    w_v, pool_v, tpool_v, mom_v,
    h1, h2, ht1, ht2, tgt,
    keep, sibs, sibr, rss, rsr,
    slope0, slope1, grad0, grad1, grad2, grad3, cur0, cur1, cur2, cur3,
    g1f, synced, drift0, drift1, fpart, frecv, fslope, final,
    zrecv, ysend, yrecv, total,
    w_sem, in_sem,
    sib_s, sib_r, rs_s, rs_r, ag_s, ag_r, agd_s, agd_r,
    f1_s, f1_r, f2_s, f2_r, z1_s, z1_r, y_s, y_r, z2_s, z2_r,
):
    tokens = rows_ref.shape[1]
    pool = pool_v.shape[0]
    depth = w_v.shape[1]
    zrows = depth // NZ
    ftok = tokens // NTP

    me = lax.axis_index("tp")
    core = lax.rem(me, 2)
    chip = lax.div(me, 2)
    cy = lax.div(chip, NX)
    cx = lax.rem(chip, NX)
    rep = lax.axis_index("rep")
    rz = lax.div(rep, 2)
    ry = lax.rem(rep, 2)
    sibling = chip * 2 + 1 - core
    frag = frag_ref[0]
    slopes = (slope0, slope1)
    drifts = (drift0, drift1)
    grads = (grad0, grad1, grad2, grad3)
    currents = (cur0, cur1, cur2, cur3)

    def chip_at(r):
        return lax.rem(cy + r // NX, 2) * NX + lax.rem(cx + r % NX * (1 + 2 * core), NX)

    def rep_at(s):
        return lax.rem(rz + s, NZ) * 2 + ry

    def loop(lo, hi, body):
        def step(i, carry):
            body(i)
            return carry

        lax.fori_loop(lo, hi, step, 0)

    def w_copy(c, r, j):
        slot = (chip_at(r) * 2 + j) * 2 + c
        return pltpu.make_async_copy(
            w_hbm.at[:, pl.ds(pl.multiple_of(slot * LANES, LANES), LANES)],
            w_v.at[slot],
            w_sem.at[c, r, j],
        )

    pool_copy = pltpu.make_async_copy(pool_hbm.at[0], pool_v, in_sem.at[0])
    tpool_copy = pltpu.make_async_copy(tpool_hbm.at[0], tpool_v, in_sem.at[1])
    mom_copy = pltpu.make_async_copy(mom_hbm, mom_v, in_sem.at[2])
    pool_copy.start()
    for c in range(2):
        for r in OUTWARD:
            w_copy(c, r, 0).start()
            w_copy(c, r, 1).start()
    tpool_copy.start()
    mom_copy.start()

    barrier = pltpu.get_barrier_semaphore()

    def greet_tp(i):
        pl.semaphore_signal(
            barrier, inc=1, device_id={"tp": lax.rem(me + i, NTP)}, device_id_type=MESH
        )

    def greet_z(i):
        pl.semaphore_signal(barrier, inc=1, device_id={"rep": rep_at(i)}, device_id_type=MESH)

    loop(1, NTP, greet_tp)
    loop(1, NZ, greet_z)
    pl.semaphore_signal(barrier, inc=1, device_id={"rep": rz * 2 + 1 - ry}, device_id_type=MESH)

    def picks(k):
        at = lax.broadcasted_iota(jnp.int32, (pool, tokens), 0)
        return jnp.where(at == rows_ref[pl.ds(k, 1), :], 1.0, 0.0).astype(BF16)

    pool_copy.wait()
    h1[...] = dot(picks(0), pool_v[...], 0, 0).astype(BF16)

    def sib_copy(u, r, to):
        return pltpu.make_async_remote_copy(
            src_ref=sibs.at[u, r], dst_ref=sibr.at[u, to],
            send_sem=sib_s.at[u, r], recv_sem=sib_r.at[u, to],
            device_id={"tp": sibling}, device_id_type=MESH,
        )

    def rs_copy(u, m):
        return pltpu.make_async_remote_copy(
            src_ref=rss.at[u, m], dst_ref=rsr.at[u, m],
            send_sem=rs_s.at[u, m], recv_sem=rs_r.at[u, m],
            device_id={"tp": chip_at(HOPS[m][2]) * 2 + core}, device_id_type=MESH,
        )

    def ag_copy(c, m):
        here, to, there = SPREAD[m]
        owner = chip_at(here) * 2 + core
        return pltpu.make_async_remote_copy(
            src_ref=slopes[c].at[owner], dst_ref=slopes[c].at[owner],
            send_sem=ag_s.at[c, m], recv_sem=ag_r.at[c, there],
            device_id={"tp": chip_at(to) * 2 + core}, device_id_type=MESH,
        )

    def ag_arrival(c, r):
        owner = chip_at(r) * 2 + core
        return pltpu.make_async_remote_copy(
            src_ref=slopes[c].at[owner], dst_ref=slopes[c].at[owner],
            send_sem=ag_s.at[c, 0], recv_sem=ag_r.at[c, r],
            device_id={"tp": sibling}, device_id_type=MESH,
        )

    def agd_copy(c, r):
        owner = chip_at(r) * 2 + core
        return pltpu.make_async_remote_copy(
            src_ref=slopes[c].at[owner], dst_ref=slopes[c].at[owner],
            send_sem=agd_s.at[c, r], recv_sem=agd_r.at[c, mirror(r)],
            device_id={"tp": sibling}, device_id_type=MESH,
        )

    def agd_arrival(c, r):
        owner = chip_at(r) * 2 + 1 - core
        return pltpu.make_async_remote_copy(
            src_ref=slopes[c].at[owner], dst_ref=slopes[c].at[owner],
            send_sem=agd_s.at[c, r], recv_sem=agd_r.at[c, r],
            device_id={"tp": sibling}, device_id_type=MESH,
        )

    def ftoks(i):
        return pl.ds(pl.multiple_of(i * ftok, ftok), ftok)

    def f1_copy(k, i):
        to = lax.rem(me + i, NTP)
        return pltpu.make_async_remote_copy(
            src_ref=fpart.at[k, :, ftoks(to), :], dst_ref=frecv.at[k, i],
            send_sem=f1_s.at[k, i], recv_sem=f1_r.at[k, i],
            device_id={"tp": to}, device_id_type=MESH,
        )

    def f2_copy(k, i):
        to = lax.rem(me + i, NTP)
        return pltpu.make_async_remote_copy(
            src_ref=fslope.at[k, :, ftoks(me), :], dst_ref=fslope.at[k, :, ftoks(me), :],
            send_sem=f2_s.at[k, i], recv_sem=f2_r.at[k, i],
            device_id={"tp": to}, device_id_type=MESH,
        )

    def zpart(i):
        return pl.ds(pl.multiple_of(i * zrows, 16), zrows)

    def z1_copy(c, s):
        return pltpu.make_async_remote_copy(
            src_ref=drifts[c].at[zpart(lax.rem(rz + s, NZ)), :], dst_ref=zrecv.at[c, s],
            send_sem=z1_s.at[c, s], recv_sem=z1_r.at[c, s],
            device_id={"rep": rep_at(s)}, device_id_type=MESH,
        )

    def y_copy(c):
        return pltpu.make_async_remote_copy(
            src_ref=ysend.at[c], dst_ref=yrecv.at[c],
            send_sem=y_s.at[c], recv_sem=y_r.at[c],
            device_id={"rep": rz * 2 + 1 - ry}, device_id_type=MESH,
        )

    def z2_copy(c, s):
        return pltpu.make_async_remote_copy(
            src_ref=total.at[c, zpart(rz), :], dst_ref=total.at[c, zpart(rz), :],
            send_sem=z2_s.at[c, s], recv_sem=z2_r.at[c, s],
            device_id={"rep": rep_at(s)}, device_id_type=MESH,
        )

    def lanes(c):
        return pl.ds(c * LANES, LANES)

    def w_pair(c, r):
        q = chip_at(r)
        mine = w_v[(q * 2 + core) * 2 + c]
        other = w_v[(q * 2 + 1 - core) * 2 + c]
        return jnp.concatenate([mine, other], axis=1)

    def hold(u, r, part):
        keep[u, r] = part[:, :LANES].astype(BF16)
        sibs[u, r] = part[:, LANES:].astype(BF16)

    def both(u, r):
        sib_copy(u, r, r).wait_recv()
        return keep[u, r].astype(F32) + sibr[u, r].astype(F32)

    def hop(u, m):
        r, added, _ = HOPS[m]
        acc = both(u, r)
        if added is not None:
            rs_copy(u, added).wait_recv()
            acc = acc + rsr[u, added].astype(F32)
        rss[u, m] = acc.astype(BF16)
        rs_copy(u, m).start()

    def hops(u, *messages):
        for m in messages:
            hop(u, m)

    def own_sum(u):
        acc = both(u, 0)
        for m in LAST_HOPS:
            rs_copy(u, m).wait_recv()
            acc = acc + rsr[u, m].astype(F32)
        return acc

    def forward_one(c, half):
        group = OUTWARD[half * 4 : half * 4 + 4]
        for r in group:
            w_copy(c, r, 0).wait()
            w_copy(c, r, 1).wait()
        for r in group:
            hold(c, r, dot(h1[...], w_pair(c, r)))
        if c == 0 and half == 0:
            pl.semaphore_wait(barrier, NTP - 1 + NZ)
        for r in group:
            sib_copy(c, r, mirror(r)).start()

    def slope_send(c):
        diff = own_sum(c) - tgt[0, :, lanes(c)].astype(F32)
        slopes[c][me] = (diff * (1.0 / tokens)).astype(BF16)
        for m in range(3):
            ag_copy(c, m).start()
        agd_copy(c, 0).start()

    def pass_on(c, *places):
        for r in places:
            ag_arrival(c, r).wait_recv()
            for m in range(3, len(SPREAD)):
                if SPREAD[m][0] == r:
                    ag_copy(c, m).start()
            agd_copy(c, r).start()

    def stage(i):
        if i < len(GROUPS):
            for c, r in GROUPS[i]:
                agd_arrival(c, r).wait_recv()
        if i >= 2:
            for j, (c, r) in enumerate(GROUPS[i - 2]):
                hold(2 + c, r, dot(h2[...], currents[i % 2 * 2 + j][...]))
        if 1 <= i <= len(GROUPS):
            for j, (c, r) in enumerate(GROUPS[i - 1]):
                at = (i - 1) % 2 * 2 + j
                w = w_pair(c, r).astype(F32)
                grad = grads[at][...]
                scale = pl.reciprocal(
                    jnp.abs(grad) * (1.0 / INNER_RATE) + ADAM_EPS / INNER_RATE, approx=True
                )
                now = w * (1.0 - INNER_RATE * DECAY_RATE) - grad * scale
                currents[at][...] = now.astype(BF16)
        if i < len(GROUPS):
            for j, (c, r) in enumerate(GROUPS[i]):
                q = chip_at(r)
                mine, other = slopes[c][q * 2 + core], slopes[c][q * 2 + 1 - core]
                grads[i % 2 * 2 + j][...] = dot(ht1[...], jnp.concatenate([mine, other], axis=1))
        if i >= 2:
            for c, r in GROUPS[i - 2]:
                sib_copy(2 + c, r, mirror(r)).start()

    def fragment_part(k, c, part):
        taken = jnp.where(frag == me, 1.0, 0.0) * tgt[k, :, lanes(c)].astype(F32)
        fpart[k, c] = (part - taken).astype(BF16)

    def fragment_forward():
        for c in range(2):
            fragment_part(0, c, dot(h1[...], w_v[frag * 2 + c]))
        loop(1, NTP, lambda i: f1_copy(0, i).start())

    def fragment_slope(k):
        acc = fpart[k, :, ftoks(me), :].astype(F32)
        for i in range(1, NTP):
            f1_copy(k, i).wait_recv()
            acc = acc + frecv[k, i].astype(F32)
        fslope[k, :, ftoks(me), :] = (acc * (1.0 / tokens)).astype(BF16)
        loop(1, NTP, lambda i: f2_copy(k, i).start())

    def fragment_one():
        loop(1, NTP, lambda i: f2_copy(0, i).wait_recv())
        for c in range(2):
            grad = dot(ht1[...], fslope[0, c])
            anchor = w_v[frag * 2 + c].astype(F32)
            ratio = grad * recip(jnp.abs(grad) + ADAM_EPS)
            after = anchor - INNER_RATE * (ratio + DECAY_RATE * anchor)
            g1f[c] = grad
            synced[c] = after
            drifts[c][...] = (anchor - after).astype(BF16)
            loop(1, NZ, lambda s, c=c: z1_copy(c, s).start())
        for c in range(2):
            fragment_part(1, c, dot(h2[...], synced[c].astype(BF16)))
        loop(1, NTP, lambda i: f1_copy(1, i).start())

    def fragment_two():
        loop(1, NTP, lambda i: f2_copy(1, i).wait_recv())
        for c in range(2):
            grad = dot(ht2[...], fslope[1, c])
            one = g1f[c]
            first = BETA_ONE * (1.0 - BETA_ONE) * one + (1.0 - BETA_ONE) * grad
            second = BETA_TWO * (1.0 - BETA_TWO) * one * one + (1.0 - BETA_TWO) * grad * grad
            ratio = (first * (1.0 / (1.0 - BETA_ONE**2))) / (
                jnp.sqrt(second * (1.0 / (1.0 - BETA_TWO**2))) + ADAM_EPS
            )
            after = synced[c]
            final[c] = after - INNER_RATE * (ratio + DECAY_RATE * after)

    def z_sum(c):
        acc = drifts[c][zpart(rz), :].astype(F32)
        for s in range(1, NZ):
            z1_copy(c, s).wait_recv()
            acc = acc + zrecv[c, s].astype(F32)
        ysend[c] = acc.astype(BF16)
        y_copy(c).start()

    def y_sum(c):
        y_copy(c).wait_recv()
        total[c, zpart(rz), :] = (ysend[c].astype(F32) + yrecv[c].astype(F32)).astype(BF16)
        loop(1, NZ, lambda s: z2_copy(c, s).start())

    def residual_out(c):
        diff = own_sum(2 + c) - tgt[1, :, lanes(c)].astype(F32)
        res_ref[0, lanes(c), :] = diff.T

    def outer(c):
        loop(1, NZ, lambda s: z2_copy(c, s).wait_recv())
        anchor = w_v[frag * 2 + c].astype(F32)
        mean = total[c].astype(F32) * (1.0 / (2 * NZ))
        moved = OUTER_MOMENTUM * mom_v[:, lanes(c)] + mean
        new = anchor - OUTER_RATE * (mean + OUTER_MOMENTUM * moved)
        nm_ref[:, lanes(c)] = moved
        ng_ref[:, lanes(c)] = new
        lf_ref[0, :, lanes(c)] = (MIX_KEEP * final[c] + (1.0 - MIX_KEEP) * new).astype(BF16)

    forward_one(0, 0)
    forward_one(0, 1)
    tpool_copy.wait()
    tgt[0] = dot(picks(0), tpool_v[...], 0, 0).astype(BF16)
    forward_one(1, 0)
    hops(0, 0, 2, 1)
    forward_one(1, 1)
    fragment_forward()
    hops(1, 0, 2, 1)
    ht1[...] = dot(pool_v[...], picks(0), 0, 0).astype(BF16)
    hops(0, 3, 4, 5)
    h2[...] = dot(picks(1), pool_v[...], 0, 0).astype(BF16)
    hops(1, 3, 4, 5)
    fragment_slope(0)
    tgt[1] = dot(picks(1), tpool_v[...], 0, 0).astype(BF16)
    hops(0, 6)
    hops(1, 6)
    ht2[...] = dot(pool_v[...], picks(1), 0, 0).astype(BF16)
    slope_send(0)
    slope_send(1)
    fragment_one()
    stage(0)
    pass_on(0, 1, 3, 4)
    pass_on(1, 1, 3, 4)
    stage(1)
    stage(2)
    pass_on(0, 5, 7, 2)
    pass_on(1, 5, 7, 2)
    stage(3)
    fragment_slope(1)
    stage(4)
    pass_on(0, 6)
    pass_on(1, 6)
    stage(5)
    stage(6)
    z_sum(0)
    stage(7)
    stage(8)
    stage(9)
    y_sum(0)
    hops(2, 2, 1)
    hops(3, 2, 1)
    z_sum(1)
    hops(2, 0)
    hops(3, 0)
    fragment_two()
    hops(2, 4, 5)
    hops(3, 4, 5)
    y_sum(1)
    hops(2, 3)
    hops(3, 3)
    mom_copy.wait()
    hops(2, 6)
    hops(3, 6)
    outer(0)
    residual_out(0)
    residual_out(1)
    outer(1)

    for u in range(4):
        for r in range(NCHIP):
            sib_copy(u, r, r).wait_send()
        for m in range(len(HOPS)):
            rs_copy(u, m).wait_send()
    for c in range(2):
        for m in range(len(SPREAD)):
            ag_copy(c, m).wait_send()
        for r in range(NCHIP):
            agd_copy(c, r).wait_send()
        loop(1, NZ, lambda s, c=c: z1_copy(c, s).wait_send())
        y_copy(c).wait_send()
        loop(1, NZ, lambda s, c=c: z2_copy(c, s).wait_send())
    for k in range(2):
        loop(1, NTP, lambda i, k=k: f1_copy(k, i).wait_send())
        loop(1, NTP, lambda i, k=k: f2_copy(k, i).wait_send())


def copy_out(*refs):
    sem = refs[-1]
    copies = [pltpu.make_async_copy(refs[i], refs[4 + i], sem.at[i]) for i in range(4)]
    for copy in copies:
        copy.start()
    for copy in copies:
        copy.wait()


def body(weights, hidden_pool, target_pool, token_rows, fragment, outer_momentum):
    depth, features = weights.shape
    pool = hidden_pool.shape[1]
    width = outer_momentum.shape[1]
    owned = target_pool.shape[2]
    tokens = token_rows.shape[2]
    zrows = depth // NZ
    blocks = features // LANES
    dma = pltpu.SemaphoreType.DMA
    scratch = [
        pltpu.VMEM((blocks, depth, LANES), BF16),
        pltpu.VMEM((pool, depth), BF16),
        pltpu.VMEM((pool, owned), BF16),
        pltpu.VMEM((depth, width), F32),
        pltpu.VMEM((tokens, depth), BF16),
        pltpu.VMEM((tokens, depth), BF16),
        pltpu.VMEM((depth, tokens), BF16),
        pltpu.VMEM((depth, tokens), BF16),
        pltpu.VMEM((2, tokens, owned), BF16),
        *[pltpu.VMEM((4, NCHIP, tokens, LANES), BF16)] * 5,
        *[pltpu.VMEM((NTP, tokens, LANES), BF16)] * 2,
        *[pltpu.VMEM((depth, 2 * LANES), F32)] * 4,
        *[pltpu.VMEM((depth, 2 * LANES), BF16)] * 4,
        pltpu.VMEM((2, depth, LANES), F32),
        pltpu.VMEM((2, depth, LANES), F32),
        *[pltpu.VMEM((depth, LANES), BF16)] * 2,
        pltpu.VMEM((2, 2, tokens, LANES), BF16),
        pltpu.VMEM((2, NTP, 2, tokens // NTP, LANES), BF16),
        pltpu.VMEM((2, 2, tokens, LANES), BF16),
        pltpu.VMEM((2, depth, LANES), F32),
        pltpu.VMEM((2, NZ, zrows, LANES), BF16),
        pltpu.VMEM((2, zrows, LANES), BF16),
        pltpu.VMEM((2, zrows, LANES), BF16),
        pltpu.VMEM((2, depth, LANES), BF16),
        dma((2, NCHIP, 2)),
        dma((3,)),
        *[dma((4, NCHIP))] * 4,
        *[dma((2, NCHIP))] * 4,
        *[dma((2, NTP))] * 4,
        dma((2, NZ)),
        dma((2, NZ)),
        dma((2,)),
        dma((2,)),
        dma((2, NZ)),
        dma((2, NZ)),
    ]
    hbm = pl.BlockSpec(memory_space=pl.ANY)
    vmem = pl.BlockSpec(memory_space=pltpu.VMEM)
    smem = pl.BlockSpec(memory_space=pltpu.SMEM)
    results = (
        jax.ShapeDtypeStruct((depth, width), F32),
        jax.ShapeDtypeStruct((depth, width), F32),
        jax.ShapeDtypeStruct((1, depth, width), BF16),
        jax.ShapeDtypeStruct((1, owned, tokens), F32),
    )
    held = pl.pallas_call(
        kernel,
        out_shape=tuple(pltpu.VMEM(r.shape, r.dtype) for r in results),
        in_specs=[hbm, hbm, hbm, vmem, smem, hbm],
        out_specs=(vmem, vmem, vmem, vmem),
        scratch_shapes=scratch,
        compiler_params=pltpu.CompilerParams(
            collective_id=0, has_side_effects=True, vmem_limit_bytes=56 * 1024 * 1024
        ),
    )(weights, hidden_pool, target_pool, token_rows[0], fragment, outer_momentum)
    return pl.pallas_call(
        copy_out,
        out_shape=results,
        in_specs=[hbm] * 4,
        out_specs=(hbm,) * 4,
        scratch_shapes=[dma((4,))],
        compiler_params=pltpu.CompilerParams(vmem_limit_bytes=4 * 1024 * 1024),
    )(*held)


def solution(mesh):
    in_specs = (
        P("tp", None),
        P("rep", None, "tp"),
        P("rep", None, "tp"),
        P("rep", None, None),
        P(),
        P("tp", None),
    )
    out_specs = (P("tp", None), P("tp", None), P("rep", "tp", None), P("rep", "tp", None))
    return jax.shard_map(body, mesh=mesh, in_specs=in_specs, out_specs=out_specs, check_vma=False)
```

```python
import functools

import jax
import jax.numpy as jnp
from jax import lax
from jax.experimental import pallas as pl
from jax.experimental.pallas import tpu as pltpu
from jax.sharding import PartitionSpec as P

BETA_ONE = 0.9
BETA_TWO = 0.95
INNER_RATE = 0.001
DECAY_RATE = 0.1
ADAM_EPS = 0.001
OUTER_RATE = 0.7
OUTER_MOMENTUM = 0.9
MIX_KEEP = 0.5

MESH = pl.DeviceIdType.MESH
F32 = jnp.float32
BF16 = jnp.bfloat16

NX = 4
NCHIP = 8
NTP = 16
NZ = 8
LANES = 128


def dot(a, b, ca=1, cb=0):
    return lax.dot_general(a, b, (((ca,), (cb,)), ((), ())), preferred_element_type=F32)


def recip(x):
    r = pl.reciprocal(x, approx=True)
    return r * (2.0 - x * r)


AHEAD, BEHIND, ACROSS = 1, NX - 1, NX
HOPS = (
    (6, None, AHEAD),
    (7, None, BEHIND),
    (2, None, BEHIND),
    (5, 0, ACROSS),
    (4, 1, ACROSS),
    (3, 2, BEHIND),
    (1, 3, AHEAD),
)
LAST_HOPS = (4, 5, 6)
SPREAD = (
    (0, AHEAD, 3),
    (0, BEHIND, 1),
    (0, ACROSS, 4),
    (1, ACROSS, 5),
    (4, AHEAD, 7),
    (3, AHEAD, 2),
    (5, BEHIND, 6),
)
OUTWARD = (6, 2, 7, 5, 4, 3, 1, 0)
FAR = 6
GROUPS = (
    ((0, 0), (1, 0)),
    ((0, 1), (0, 3)),
    ((0, 4), (1, 1)),
    ((1, 3), (1, 4)),
    ((0, 5), (0, 7)),
    ((0, 2), (1, 5)),
    ((1, 7), (1, 2)),
    ((0, 6), (1, 6)),
)


def mirror(r):
    return r // NX * NX + (NX - r % NX) % NX


def kernel(
    w_hbm, pool_hbm, tpool_hbm, rows_ref, frag_ref, mom_hbm,
    nm_ref, ng_ref, lf_ref, res_ref,
    w_v, pool_v, tpool_v, mom_v,
    h1, h2, ht1, ht2, tgt,
    keep, sibs, sibr, rss, rsr,
    slope0, slope1, grad0, grad1, grad2, grad3, cur0, cur1, cur2, cur3,
    g1f, synced, drift0, drift1, fpart, frecv, fslope, final,
    zrecv, ysend, yrecv, total,
    w_sem, in_sem,
    sib_s, sib_r, rs_s, rs_r, ag_s, ag_r, agd_s, agd_r,
    f1_s, f1_r, f2_s, f2_r, z1_s, z1_r, y_s, y_r, z2_s, z2_r,
):
    tokens = rows_ref.shape[1]
    pool = pool_v.shape[0]
    depth = w_v.shape[1]
    zrows = depth // NZ
    ftok = tokens // NTP

    me = lax.axis_index("tp")
    core = lax.rem(me, 2)
    chip = lax.div(me, 2)
    cy = lax.div(chip, NX)
    cx = lax.rem(chip, NX)
    rep = lax.axis_index("rep")
    rz = lax.div(rep, 2)
    ry = lax.rem(rep, 2)
    sibling = chip * 2 + 1 - core
    frag = frag_ref[0]
    slopes = (slope0, slope1)
    drifts = (drift0, drift1)
    grads = (grad0, grad1, grad2, grad3)
    currents = (cur0, cur1, cur2, cur3)

    def chip_at(r):
        return lax.rem(cy + r // NX, 2) * NX + lax.rem(cx + r % NX * (1 + 2 * core), NX)

    def rep_at(s):
        return lax.rem(rz + s, NZ) * 2 + ry

    def loop(lo, hi, body):
        def step(i, carry):
            body(i)
            return carry

        lax.fori_loop(lo, hi, step, 0)

    def w_copy(c, r, j):
        slot = (chip_at(r) * 2 + j) * 2 + c
        return pltpu.make_async_copy(
            w_hbm.at[:, pl.ds(pl.multiple_of(slot * LANES, LANES), LANES)],
            w_v.at[slot],
            w_sem.at[c, r, j],
        )

    pool_copy = pltpu.make_async_copy(pool_hbm.at[0], pool_v, in_sem.at[0])
    tpool_copy = pltpu.make_async_copy(tpool_hbm.at[0], tpool_v, in_sem.at[1])
    mom_copy = pltpu.make_async_copy(mom_hbm, mom_v, in_sem.at[2])
    pool_copy.start()
    for c in range(2):
        for r in OUTWARD:
            w_copy(c, r, 0).start()
            w_copy(c, r, 1).start()
    tpool_copy.start()
    mom_copy.start()

    barrier = pltpu.get_barrier_semaphore()

    def greet_tp(i):
        pl.semaphore_signal(
            barrier, inc=1, device_id={"tp": lax.rem(me + i, NTP)}, device_id_type=MESH
        )

    def greet_z(i):
        pl.semaphore_signal(barrier, inc=1, device_id={"rep": rep_at(i)}, device_id_type=MESH)

    loop(1, NTP, greet_tp)
    loop(1, NZ, greet_z)
    pl.semaphore_signal(barrier, inc=1, device_id={"rep": rz * 2 + 1 - ry}, device_id_type=MESH)

    def picks(k):
        at = lax.broadcasted_iota(jnp.int32, (pool, tokens), 0)
        return jnp.where(at == rows_ref[pl.ds(k, 1), :], 1.0, 0.0).astype(BF16)

    pool_copy.wait()
    h1[...] = dot(picks(0), pool_v[...], 0, 0).astype(BF16)

    def sib_copy(u, r, to):
        return pltpu.make_async_remote_copy(
            src_ref=sibs.at[u, r], dst_ref=sibr.at[u, to],
            send_sem=sib_s.at[u, r], recv_sem=sib_r.at[u, to],
            device_id={"tp": sibling}, device_id_type=MESH,
        )

    def far_copy(u):
        return pltpu.make_async_remote_copy(
            src_ref=sibs.at[u, FAR], dst_ref=sibr.at[u, FAR],
            send_sem=sib_s.at[u, FAR], recv_sem=sib_r.at[u, FAR],
            device_id={"tp": chip_at(BEHIND) * 2 + 1 - core}, device_id_type=MESH,
        )

    def rs_copy(u, m):
        return pltpu.make_async_remote_copy(
            src_ref=keep.at[u, FAR] if m == 0 else rss.at[u, m], dst_ref=rsr.at[u, m],
            send_sem=rs_s.at[u, m], recv_sem=rs_r.at[u, m],
            device_id={"tp": chip_at(HOPS[m][2]) * 2 + core}, device_id_type=MESH,
        )

    def ag_copy(c, m):
        here, to, there = SPREAD[m]
        owner = chip_at(here) * 2 + core
        return pltpu.make_async_remote_copy(
            src_ref=slopes[c].at[owner], dst_ref=slopes[c].at[owner],
            send_sem=ag_s.at[c, m], recv_sem=ag_r.at[c, there],
            device_id={"tp": chip_at(to) * 2 + core}, device_id_type=MESH,
        )

    def ag_arrival(c, r):
        owner = chip_at(r) * 2 + core
        return pltpu.make_async_remote_copy(
            src_ref=slopes[c].at[owner], dst_ref=slopes[c].at[owner],
            send_sem=ag_s.at[c, 0], recv_sem=ag_r.at[c, r],
            device_id={"tp": sibling}, device_id_type=MESH,
        )

    def agd_copy(c, r):
        owner = chip_at(r) * 2 + core
        return pltpu.make_async_remote_copy(
            src_ref=slopes[c].at[owner], dst_ref=slopes[c].at[owner],
            send_sem=agd_s.at[c, r], recv_sem=agd_r.at[c, mirror(r)],
            device_id={"tp": sibling}, device_id_type=MESH,
        )

    def ag_far(c):
        owner = chip_at(5) * 2 + core
        return pltpu.make_async_remote_copy(
            src_ref=slopes[c].at[owner], dst_ref=slopes[c].at[owner],
            send_sem=agd_s.at[c, FAR], recv_sem=agd_r.at[c, FAR],
            device_id={"tp": chip_at(BEHIND) * 2 + 1 - core}, device_id_type=MESH,
        )

    def agd_arrival(c, r):
        owner = chip_at(r) * 2 + 1 - core
        return pltpu.make_async_remote_copy(
            src_ref=slopes[c].at[owner], dst_ref=slopes[c].at[owner],
            send_sem=agd_s.at[c, r], recv_sem=agd_r.at[c, r],
            device_id={"tp": sibling}, device_id_type=MESH,
        )

    def ftoks(i):
        return pl.ds(pl.multiple_of(i * ftok, ftok), ftok)

    def f1_copy(k, i):
        to = lax.rem(me + i, NTP)
        return pltpu.make_async_remote_copy(
            src_ref=fpart.at[k, :, ftoks(to), :], dst_ref=frecv.at[k, i],
            send_sem=f1_s.at[k, i], recv_sem=f1_r.at[k, i],
            device_id={"tp": to}, device_id_type=MESH,
        )

    def f2_copy(k, i):
        to = lax.rem(me + i, NTP)
        return pltpu.make_async_remote_copy(
            src_ref=fslope.at[k, :, ftoks(me), :], dst_ref=fslope.at[k, :, ftoks(me), :],
            send_sem=f2_s.at[k, i], recv_sem=f2_r.at[k, i],
            device_id={"tp": to}, device_id_type=MESH,
        )

    def zpart(i):
        return pl.ds(pl.multiple_of(i * zrows, 16), zrows)

    def z1_copy(c, s):
        return pltpu.make_async_remote_copy(
            src_ref=drifts[c].at[zpart(lax.rem(rz + s, NZ)), :], dst_ref=zrecv.at[c, s],
            send_sem=z1_s.at[c, s], recv_sem=z1_r.at[c, s],
            device_id={"rep": rep_at(s)}, device_id_type=MESH,
        )

    def y_copy(c):
        return pltpu.make_async_remote_copy(
            src_ref=ysend.at[c], dst_ref=yrecv.at[c],
            send_sem=y_s.at[c], recv_sem=y_r.at[c],
            device_id={"rep": rz * 2 + 1 - ry}, device_id_type=MESH,
        )

    def z2_copy(c, s):
        return pltpu.make_async_remote_copy(
            src_ref=total.at[c, zpart(rz), :], dst_ref=total.at[c, zpart(rz), :],
            send_sem=z2_s.at[c, s], recv_sem=z2_r.at[c, s],
            device_id={"rep": rep_at(s)}, device_id_type=MESH,
        )

    def lanes(c):
        return pl.ds(c * LANES, LANES)

    def w_pair(c, r):
        q = chip_at(r)
        mine = w_v[(q * 2 + core) * 2 + c]
        other = w_v[(q * 2 + 1 - core) * 2 + c]
        return jnp.concatenate([mine, other], axis=1)

    def hold(u, r, part):
        keep[u, r] = part[:, :LANES].astype(BF16)
        sibs[u, r] = part[:, LANES:].astype(BF16)

    def both(u, r):
        sib_copy(u, r, r).wait_recv()
        return keep[u, r].astype(F32) + sibr[u, r].astype(F32)

    def send_partial(u, r):
        if r == FAR:
            rs_copy(u, 0).start()
            far_copy(u).start()
        else:
            sib_copy(u, r, mirror(r)).start()

    def hop(u, m):
        r, added, _ = HOPS[m]
        acc = both(u, r)
        if added == 0:
            far_copy(u).wait_recv()
            acc = acc + sibr[u, FAR].astype(F32)
        if added is not None:
            rs_copy(u, added).wait_recv()
            acc = acc + rsr[u, added].astype(F32)
        rss[u, m] = acc.astype(BF16)
        rs_copy(u, m).start()

    def hops(u, *messages):
        for m in messages:
            hop(u, m)

    def own_sum(u):
        acc = both(u, 0)
        for m in LAST_HOPS:
            rs_copy(u, m).wait_recv()
            acc = acc + rsr[u, m].astype(F32)
        return acc

    def forward_one(c, half):
        group = OUTWARD[half * 4 : half * 4 + 4]
        for r in group:
            w_copy(c, r, 0).wait()
            w_copy(c, r, 1).wait()
        for r in group:
            hold(c, r, dot(h1[...], w_pair(c, r)))
        if c == 0 and half == 0:
            pl.semaphore_wait(barrier, NTP - 1 + NZ)
        for r in group:
            send_partial(c, r)

    def slope_send(c):
        diff = own_sum(c) - tgt[0, :, lanes(c)].astype(F32)
        slopes[c][me] = (diff * (1.0 / tokens)).astype(BF16)
        for m in range(3):
            ag_copy(c, m).start()
        agd_copy(c, 0).start()

    def pass_on(c, *places):
        for r in places:
            ag_arrival(c, r).wait_recv()
            for m in range(3, len(SPREAD)):
                if SPREAD[m][0] == r:
                    ag_copy(c, m).start()
            if r == 5:
                ag_far(c).start()
            if r != FAR:
                agd_copy(c, r).start()

    def stage(i):
        if i < len(GROUPS):
            for c, r in GROUPS[i]:
                agd_arrival(c, r).wait_recv()
        if i >= 2:
            for j, (c, r) in enumerate(GROUPS[i - 2]):
                hold(2 + c, r, dot(h2[...], currents[i % 2 * 2 + j][...]))
        if 1 <= i <= len(GROUPS):
            for j, (c, r) in enumerate(GROUPS[i - 1]):
                at = (i - 1) % 2 * 2 + j
                w = w_pair(c, r).astype(F32)
                grad = grads[at][...]
                scale = pl.reciprocal(
                    jnp.abs(grad) * (1.0 / INNER_RATE) + ADAM_EPS / INNER_RATE, approx=True
                )
                now = w * (1.0 - INNER_RATE * DECAY_RATE) - grad * scale
                currents[at][...] = now.astype(BF16)
        if i < len(GROUPS):
            for j, (c, r) in enumerate(GROUPS[i]):
                q = chip_at(r)
                mine, other = slopes[c][q * 2 + core], slopes[c][q * 2 + 1 - core]
                grads[i % 2 * 2 + j][...] = dot(ht1[...], jnp.concatenate([mine, other], axis=1))
        if i >= 2:
            for c, r in GROUPS[i - 2]:
                send_partial(2 + c, r)

    def fragment_part(k, c, part):
        taken = jnp.where(frag == me, 1.0, 0.0) * tgt[k, :, lanes(c)].astype(F32)
        fpart[k, c] = (part - taken).astype(BF16)

    def fragment_forward():
        for c in range(2):
            fragment_part(0, c, dot(h1[...], w_v[frag * 2 + c]))
        loop(1, NTP, lambda i: f1_copy(0, i).start())

    def fragment_slope(k):
        acc = fpart[k, :, ftoks(me), :].astype(F32)
        for i in range(1, NTP):
            f1_copy(k, i).wait_recv()
            acc = acc + frecv[k, i].astype(F32)
        fslope[k, :, ftoks(me), :] = (acc * (1.0 / tokens)).astype(BF16)
        loop(1, NTP, lambda i: f2_copy(k, i).start())

    def fragment_one():
        loop(1, NTP, lambda i: f2_copy(0, i).wait_recv())
        for c in range(2):
            grad = dot(ht1[...], fslope[0, c])
            anchor = w_v[frag * 2 + c].astype(F32)
            ratio = grad * recip(jnp.abs(grad) + ADAM_EPS)
            after = anchor - INNER_RATE * (ratio + DECAY_RATE * anchor)
            g1f[c] = grad
            synced[c] = after
            drifts[c][...] = (anchor - after).astype(BF16)
            loop(1, NZ, lambda s, c=c: z1_copy(c, s).start())
        for c in range(2):
            fragment_part(1, c, dot(h2[...], synced[c].astype(BF16)))
        loop(1, NTP, lambda i: f1_copy(1, i).start())

    def fragment_two():
        loop(1, NTP, lambda i: f2_copy(1, i).wait_recv())
        for c in range(2):
            grad = dot(ht2[...], fslope[1, c])
            one = g1f[c]
            first = BETA_ONE * (1.0 - BETA_ONE) * one + (1.0 - BETA_ONE) * grad
            second = BETA_TWO * (1.0 - BETA_TWO) * one * one + (1.0 - BETA_TWO) * grad * grad
            ratio = (first * (1.0 / (1.0 - BETA_ONE**2))) / (
                jnp.sqrt(second * (1.0 / (1.0 - BETA_TWO**2))) + ADAM_EPS
            )
            after = synced[c]
            final[c] = after - INNER_RATE * (ratio + DECAY_RATE * after)

    def z_sum(c):
        acc = drifts[c][zpart(rz), :].astype(F32)
        for s in range(1, NZ):
            z1_copy(c, s).wait_recv()
            acc = acc + zrecv[c, s].astype(F32)
        ysend[c] = acc.astype(BF16)
        y_copy(c).start()

    def y_sum(c):
        y_copy(c).wait_recv()
        total[c, zpart(rz), :] = (ysend[c].astype(F32) + yrecv[c].astype(F32)).astype(BF16)
        loop(1, NZ, lambda s: z2_copy(c, s).start())

    def residual_out(c):
        diff = own_sum(2 + c) - tgt[1, :, lanes(c)].astype(F32)
        res_ref[0, lanes(c), :] = diff.T

    def outer(c):
        loop(1, NZ, lambda s: z2_copy(c, s).wait_recv())
        anchor = w_v[frag * 2 + c].astype(F32)
        mean = total[c].astype(F32) * (1.0 / (2 * NZ))
        moved = OUTER_MOMENTUM * mom_v[:, lanes(c)] + mean
        new = anchor - OUTER_RATE * (mean + OUTER_MOMENTUM * moved)
        nm_ref[:, lanes(c)] = moved
        ng_ref[:, lanes(c)] = new
        lf_ref[0, :, lanes(c)] = (MIX_KEEP * final[c] + (1.0 - MIX_KEEP) * new).astype(BF16)

    forward_one(0, 0)
    forward_one(0, 1)
    tpool_copy.wait()
    tgt[0] = dot(picks(0), tpool_v[...], 0, 0).astype(BF16)
    forward_one(1, 0)
    hops(0, 2, 1)
    forward_one(1, 1)
    fragment_forward()
    hops(1, 2, 1)
    ht1[...] = dot(pool_v[...], picks(0), 0, 0).astype(BF16)
    hops(0, 3, 4, 5)
    fragment_slope(0)
    hops(1, 3, 4, 5)
    h2[...] = dot(picks(1), pool_v[...], 0, 0).astype(BF16)
    tgt[1] = dot(picks(1), tpool_v[...], 0, 0).astype(BF16)
    hops(0, 6)
    hops(1, 6)
    fragment_one()
    slope_send(0)
    slope_send(1)
    ht2[...] = dot(pool_v[...], picks(1), 0, 0).astype(BF16)
    stage(0)
    pass_on(0, 1, 3, 4)
    pass_on(1, 1, 3, 4)
    fragment_slope(1)
    stage(1)
    stage(2)
    pass_on(0, 5, 7, 2)
    pass_on(1, 5, 7, 2)
    stage(3)
    z_sum(0)
    stage(4)
    stage(5)
    pass_on(0, 6)
    pass_on(1, 6)
    stage(6)
    stage(7)
    stage(8)
    stage(9)
    y_sum(0)
    hops(2, 2, 1)
    hops(3, 2, 1)
    z_sum(1)
    fragment_two()
    hops(2, 3, 4, 5)
    hops(3, 3, 4, 5)
    y_sum(1)
    mom_copy.wait()
    hops(2, 6)
    hops(3, 6)
    outer(0)
    residual_out(0)
    residual_out(1)
    outer(1)

    for u in range(4):
        for r in range(NCHIP):
            sib_copy(u, r, r).wait_send()
        for m in range(len(HOPS)):
            rs_copy(u, m).wait_send()
    for c in range(2):
        for m in range(len(SPREAD)):
            ag_copy(c, m).wait_send()
        for r in range(NCHIP):
            agd_copy(c, r).wait_send()
        loop(1, NZ, lambda s, c=c: z1_copy(c, s).wait_send())
        y_copy(c).wait_send()
        loop(1, NZ, lambda s, c=c: z2_copy(c, s).wait_send())
    for k in range(2):
        loop(1, NTP, lambda i, k=k: f1_copy(k, i).wait_send())
        loop(1, NTP, lambda i, k=k: f2_copy(k, i).wait_send())


def copy_out(*refs):
    sem = refs[-1]
    copies = [pltpu.make_async_copy(refs[i], refs[4 + i], sem.at[i]) for i in range(4)]
    for copy in copies:
        copy.start()
    for copy in copies:
        copy.wait()


def body(weights, hidden_pool, target_pool, token_rows, fragment, outer_momentum):
    depth, features = weights.shape
    pool = hidden_pool.shape[1]
    width = outer_momentum.shape[1]
    owned = target_pool.shape[2]
    tokens = token_rows.shape[2]
    zrows = depth // NZ
    blocks = features // LANES
    dma = pltpu.SemaphoreType.DMA
    scratch = [
        pltpu.VMEM((blocks, depth, LANES), BF16),
        pltpu.VMEM((pool, depth), BF16),
        pltpu.VMEM((pool, owned), BF16),
        pltpu.VMEM((depth, width), F32),
        pltpu.VMEM((tokens, depth), BF16),
        pltpu.VMEM((tokens, depth), BF16),
        pltpu.VMEM((depth, tokens), BF16),
        pltpu.VMEM((depth, tokens), BF16),
        pltpu.VMEM((2, tokens, owned), BF16),
        *[pltpu.VMEM((4, NCHIP, tokens, LANES), BF16)] * 5,
        *[pltpu.VMEM((NTP, tokens, LANES), BF16)] * 2,
        *[pltpu.VMEM((depth, 2 * LANES), F32)] * 4,
        *[pltpu.VMEM((depth, 2 * LANES), BF16)] * 4,
        pltpu.VMEM((2, depth, LANES), F32),
        pltpu.VMEM((2, depth, LANES), F32),
        *[pltpu.VMEM((depth, LANES), BF16)] * 2,
        pltpu.VMEM((2, 2, tokens, LANES), BF16),
        pltpu.VMEM((2, NTP, 2, tokens // NTP, LANES), BF16),
        pltpu.VMEM((2, 2, tokens, LANES), BF16),
        pltpu.VMEM((2, depth, LANES), F32),
        pltpu.VMEM((2, NZ, zrows, LANES), BF16),
        pltpu.VMEM((2, zrows, LANES), BF16),
        pltpu.VMEM((2, zrows, LANES), BF16),
        pltpu.VMEM((2, depth, LANES), BF16),
        dma((2, NCHIP, 2)),
        dma((3,)),
        *[dma((4, NCHIP))] * 4,
        *[dma((2, NCHIP))] * 4,
        *[dma((2, NTP))] * 4,
        dma((2, NZ)),
        dma((2, NZ)),
        dma((2,)),
        dma((2,)),
        dma((2, NZ)),
        dma((2, NZ)),
    ]
    hbm = pl.BlockSpec(memory_space=pl.ANY)
    vmem = pl.BlockSpec(memory_space=pltpu.VMEM)
    smem = pl.BlockSpec(memory_space=pltpu.SMEM)
    results = (
        jax.ShapeDtypeStruct((depth, width), F32),
        jax.ShapeDtypeStruct((depth, width), F32),
        jax.ShapeDtypeStruct((1, depth, width), BF16),
        jax.ShapeDtypeStruct((1, owned, tokens), F32),
    )
    held = pl.pallas_call(
        kernel,
        out_shape=tuple(pltpu.VMEM(r.shape, r.dtype) for r in results),
        in_specs=[hbm, hbm, hbm, vmem, smem, hbm],
        out_specs=(vmem, vmem, vmem, vmem),
        scratch_shapes=scratch,
        compiler_params=pltpu.CompilerParams(
            collective_id=0, has_side_effects=True, vmem_limit_bytes=56 * 1024 * 1024
        ),
    )(weights, hidden_pool, target_pool, token_rows[0], fragment, outer_momentum)
    return pl.pallas_call(
        copy_out,
        out_shape=results,
        in_specs=[hbm] * 4,
        out_specs=(hbm,) * 4,
        scratch_shapes=[dma((4,))],
        compiler_params=pltpu.CompilerParams(vmem_limit_bytes=4 * 1024 * 1024),
    )(*held)


def solution(mesh):
    in_specs = (
        P("tp", None),
        P("rep", None, "tp"),
        P("rep", None, "tp"),
        P("rep", None, None),
        P(),
        P("tp", None),
    )
    out_specs = (P("tp", None), P("tp", None), P("rep", "tp", None), P("rep", "tp", None))
    return jax.shard_map(body, mesh=mesh, in_specs=in_specs, out_specs=out_specs, check_vma=False)
```

```python
import functools

import jax
import jax.numpy as jnp
from jax import lax
from jax.experimental import pallas as pl
from jax.experimental.pallas import tpu as pltpu
from jax.sharding import PartitionSpec as P

BETA_ONE = 0.9
BETA_TWO = 0.95
INNER_RATE = 0.001
DECAY_RATE = 0.1
ADAM_EPS = 0.001
OUTER_RATE = 0.7
OUTER_MOMENTUM = 0.9
MIX_KEEP = 0.5

MESH = pl.DeviceIdType.MESH
F32 = jnp.float32
BF16 = jnp.bfloat16

NX = 4
NCHIP = 8
NTP = 16
NZ = 8
LANES = 128


def dot(a, b, ca=1, cb=0):
    return lax.dot_general(a, b, (((ca,), (cb,)), ((), ())), preferred_element_type=F32)


def recip(x):
    r = pl.reciprocal(x, approx=True)
    return r * (2.0 - x * r)


AHEAD, BEHIND, ACROSS = 1, NX - 1, NX
HOPS = (
    (6, None, AHEAD),
    (7, None, BEHIND),
    (2, None, BEHIND),
    (5, 0, ACROSS),
    (4, 1, ACROSS),
    (3, 2, BEHIND),
    (1, 3, AHEAD),
)
LAST_HOPS = (4, 5, 6)
SPREAD = (
    (0, AHEAD, 3),
    (0, BEHIND, 1),
    (0, ACROSS, 4),
    (1, ACROSS, 5),
    (4, AHEAD, 7),
    (3, AHEAD, 2),
    (5, BEHIND, 6),
)
OUTWARD = (6, 2, 7, 5, 4, 3, 1, 0)
FAR = 6
GROUPS = (
    ((0, 0), (1, 0)),
    ((0, 1), (0, 3)),
    ((0, 4), (1, 1)),
    ((1, 3), (1, 4)),
    ((0, 5), (0, 7)),
    ((0, 2), (1, 5)),
    ((1, 7), (1, 2)),
    ((0, 6), (1, 6)),
)


def mirror(r):
    return r // NX * NX + (NX - r % NX) % NX


def kernel(
    w_hbm, pool_hbm, tpool_hbm, rows_ref, frag_ref, mom_hbm,
    nm_ref, ng_ref, lf_ref, res_ref,
    w_v, pool_v, tpool_v, mom_v,
    h1, h2, ht1, ht2, tgt,
    keep, sibs, sibr, rss, rsr,
    slope0, slope1, grad0, grad1, grad2, grad3, cur0, cur1, cur2, cur3,
    g1f, synced, drift0, drift1, fpart, frecv, fslope, final,
    zrecv, ysend, yrecv, total,
    w_sem, in_sem,
    sib_s, sib_r, rs_s, rs_r, ag_s, ag_r, agd_s, agd_r,
    f1_s, f1_r, f2_s, f2_r, z1_s, z1_r, y_s, y_r, z2_s, z2_r,
):
    tokens = rows_ref.shape[1]
    pool = pool_v.shape[0]
    depth = w_v.shape[1]
    zrows = depth // NZ
    ftok = tokens // NTP

    me = lax.axis_index("tp")
    core = lax.rem(me, 2)
    chip = lax.div(me, 2)
    cy = lax.div(chip, NX)
    cx = lax.rem(chip, NX)
    rep = lax.axis_index("rep")
    rz = lax.div(rep, 2)
    ry = lax.rem(rep, 2)
    sibling = chip * 2 + 1 - core
    frag = frag_ref[0]
    slopes = (slope0, slope1)
    drifts = (drift0, drift1)
    grads = (grad0, grad1, grad2, grad3)
    currents = (cur0, cur1, cur2, cur3)

    def chip_at(r):
        return lax.rem(cy + r // NX, 2) * NX + lax.rem(cx + r % NX * (1 + 2 * core), NX)

    def rep_at(s):
        return lax.rem(rz + s, NZ) * 2 + ry

    def loop(lo, hi, body):
        def step(i, carry):
            body(i)
            return carry

        lax.fori_loop(lo, hi, step, 0)

    def w_copy(c, r, j):
        slot = (chip_at(r) * 2 + j) * 2 + c
        return pltpu.make_async_copy(
            w_hbm.at[:, pl.ds(pl.multiple_of(slot * LANES, LANES), LANES)],
            w_v.at[slot],
            w_sem.at[c, r, j],
        )

    pool_copy = pltpu.make_async_copy(pool_hbm.at[0], pool_v, in_sem.at[0])
    tpool_copy = pltpu.make_async_copy(tpool_hbm.at[0], tpool_v, in_sem.at[1])
    mom_copy = pltpu.make_async_copy(mom_hbm, mom_v, in_sem.at[2])
    pool_copy.start()
    for c in range(2):
        for r in OUTWARD:
            w_copy(c, r, 0).start()
            w_copy(c, r, 1).start()
    tpool_copy.start()
    mom_copy.start()

    barrier = pltpu.get_barrier_semaphore()

    def greet_tp(i):
        pl.semaphore_signal(
            barrier, inc=1, device_id={"tp": lax.rem(me + i, NTP)}, device_id_type=MESH
        )

    def greet_z(i):
        pl.semaphore_signal(barrier, inc=1, device_id={"rep": rep_at(i)}, device_id_type=MESH)

    loop(1, NTP, greet_tp)
    loop(1, NZ, greet_z)
    pl.semaphore_signal(barrier, inc=1, device_id={"rep": rz * 2 + 1 - ry}, device_id_type=MESH)

    def picks(k):
        at = lax.broadcasted_iota(jnp.int32, (pool, tokens), 0)
        return jnp.where(at == rows_ref[pl.ds(k, 1), :], 1.0, 0.0).astype(BF16)

    pool_copy.wait()
    h1[...] = dot(picks(0), pool_v[...], 0, 0).astype(BF16)

    def sib_copy(u, r, to):
        return pltpu.make_async_remote_copy(
            src_ref=sibs.at[u, r], dst_ref=sibr.at[u, to],
            send_sem=sib_s.at[u, r], recv_sem=sib_r.at[u, to],
            device_id={"tp": sibling}, device_id_type=MESH,
        )

    def far_copy(u):
        return pltpu.make_async_remote_copy(
            src_ref=sibs.at[u, FAR], dst_ref=sibr.at[u, FAR],
            send_sem=sib_s.at[u, FAR], recv_sem=sib_r.at[u, FAR],
            device_id={"tp": chip_at(BEHIND) * 2 + 1 - core}, device_id_type=MESH,
        )

    def rs_copy(u, m):
        return pltpu.make_async_remote_copy(
            src_ref=keep.at[u, FAR] if m == 0 else rss.at[u, m], dst_ref=rsr.at[u, m],
            send_sem=rs_s.at[u, m], recv_sem=rs_r.at[u, m],
            device_id={"tp": chip_at(HOPS[m][2]) * 2 + core}, device_id_type=MESH,
        )

    def ag_copy(c, m):
        here, to, there = SPREAD[m]
        owner = chip_at(here) * 2 + core
        return pltpu.make_async_remote_copy(
            src_ref=slopes[c].at[owner], dst_ref=slopes[c].at[owner],
            send_sem=ag_s.at[c, m], recv_sem=ag_r.at[c, there],
            device_id={"tp": chip_at(to) * 2 + core}, device_id_type=MESH,
        )

    def ag_arrival(c, r):
        owner = chip_at(r) * 2 + core
        return pltpu.make_async_remote_copy(
            src_ref=slopes[c].at[owner], dst_ref=slopes[c].at[owner],
            send_sem=ag_s.at[c, 0], recv_sem=ag_r.at[c, r],
            device_id={"tp": sibling}, device_id_type=MESH,
        )

    def agd_copy(c, r):
        owner = chip_at(r) * 2 + core
        return pltpu.make_async_remote_copy(
            src_ref=slopes[c].at[owner], dst_ref=slopes[c].at[owner],
            send_sem=agd_s.at[c, r], recv_sem=agd_r.at[c, mirror(r)],
            device_id={"tp": sibling}, device_id_type=MESH,
        )

    def ag_far(c):
        owner = chip_at(5) * 2 + core
        return pltpu.make_async_remote_copy(
            src_ref=slopes[c].at[owner], dst_ref=slopes[c].at[owner],
            send_sem=agd_s.at[c, FAR], recv_sem=agd_r.at[c, FAR],
            device_id={"tp": chip_at(BEHIND) * 2 + 1 - core}, device_id_type=MESH,
        )

    def agd_arrival(c, r):
        owner = chip_at(r) * 2 + 1 - core
        return pltpu.make_async_remote_copy(
            src_ref=slopes[c].at[owner], dst_ref=slopes[c].at[owner],
            send_sem=agd_s.at[c, r], recv_sem=agd_r.at[c, r],
            device_id={"tp": sibling}, device_id_type=MESH,
        )

    def ftoks(i):
        return pl.ds(pl.multiple_of(i * ftok, ftok), ftok)

    def f1_copy(k, i):
        to = lax.rem(me + i, NTP)
        return pltpu.make_async_remote_copy(
            src_ref=fpart.at[k, :, ftoks(to), :], dst_ref=frecv.at[k, i],
            send_sem=f1_s.at[k, i], recv_sem=f1_r.at[k, i],
            device_id={"tp": to}, device_id_type=MESH,
        )

    def f2_copy(k, i):
        to = lax.rem(me + i, NTP)
        return pltpu.make_async_remote_copy(
            src_ref=fslope.at[k, :, ftoks(me), :], dst_ref=fslope.at[k, :, ftoks(me), :],
            send_sem=f2_s.at[k, i], recv_sem=f2_r.at[k, i],
            device_id={"tp": to}, device_id_type=MESH,
        )

    def zpart(i):
        return pl.ds(pl.multiple_of(i * zrows, 16), zrows)

    def z1_copy(c, s):
        return pltpu.make_async_remote_copy(
            src_ref=drifts[c].at[zpart(lax.rem(rz + s, NZ)), :], dst_ref=zrecv.at[c, s],
            send_sem=z1_s.at[c, s], recv_sem=z1_r.at[c, s],
            device_id={"rep": rep_at(s)}, device_id_type=MESH,
        )

    def y_copy(c):
        return pltpu.make_async_remote_copy(
            src_ref=ysend.at[c], dst_ref=yrecv.at[c],
            send_sem=y_s.at[c], recv_sem=y_r.at[c],
            device_id={"rep": rz * 2 + 1 - ry}, device_id_type=MESH,
        )

    def z2_copy(c, s):
        return pltpu.make_async_remote_copy(
            src_ref=total.at[c, zpart(rz), :], dst_ref=total.at[c, zpart(rz), :],
            send_sem=z2_s.at[c, s], recv_sem=z2_r.at[c, s],
            device_id={"rep": rep_at(s)}, device_id_type=MESH,
        )

    def lanes(c):
        return pl.ds(c * LANES, LANES)

    def w_pair(c, r):
        q = chip_at(r)
        mine = w_v[(q * 2 + core) * 2 + c]
        other = w_v[(q * 2 + 1 - core) * 2 + c]
        return jnp.concatenate([mine, other], axis=1)

    def hold(u, r, part):
        keep[u, r] = part[:, :LANES].astype(BF16)
        sibs[u, r] = part[:, LANES:].astype(BF16)

    def both(u, r):
        sib_copy(u, r, r).wait_recv()
        return keep[u, r].astype(F32) + sibr[u, r].astype(F32)

    def send_partial(u, r):
        if r == FAR:
            rs_copy(u, 0).start()
            far_copy(u).start()
        else:
            sib_copy(u, r, mirror(r)).start()

    def hop(u, m):
        r, added, _ = HOPS[m]
        acc = both(u, r)
        if added == 0:
            far_copy(u).wait_recv()
            acc = acc + sibr[u, FAR].astype(F32)
        if added is not None:
            rs_copy(u, added).wait_recv()
            acc = acc + rsr[u, added].astype(F32)
        rss[u, m] = acc.astype(BF16)
        rs_copy(u, m).start()

    def hops(u, *messages):
        for m in messages:
            hop(u, m)

    def own_sum(u):
        acc = both(u, 0)
        for m in LAST_HOPS:
            rs_copy(u, m).wait_recv()
            acc = acc + rsr[u, m].astype(F32)
        return acc

    def forward_one(c, half):
        group = OUTWARD[half * 4 : half * 4 + 4]
        for r in group:
            w_copy(c, r, 0).wait()
            w_copy(c, r, 1).wait()
        for r in group:
            hold(c, r, dot(h1[...], w_pair(c, r)))
        if c == 0 and half == 0:
            pl.semaphore_wait(barrier, NTP - 1 + NZ)
        for r in group:
            send_partial(c, r)

    def slope_send(c):
        diff = own_sum(c) - tgt[0, :, lanes(c)].astype(F32)
        slopes[c][me] = (diff * (1.0 / tokens)).astype(BF16)
        for m in range(3):
            ag_copy(c, m).start()
        agd_copy(c, 0).start()

    def pass_on(c, *places):
        for r in places:
            ag_arrival(c, r).wait_recv()
            for m in range(3, len(SPREAD)):
                if SPREAD[m][0] == r:
                    ag_copy(c, m).start()
            if r == 5:
                ag_far(c).start()
            if r != FAR:
                agd_copy(c, r).start()

    def columns_arrive(i):
        for c, r in GROUPS[i]:
            agd_arrival(c, r).wait_recv()

    def columns_gradient(i):
        for j, (c, r) in enumerate(GROUPS[i]):
            q = chip_at(r)
            mine, other = slopes[c][q * 2 + core], slopes[c][q * 2 + 1 - core]
            grads[i % 2 * 2 + j][...] = dot(ht1[...], jnp.concatenate([mine, other], axis=1))

    def columns_adamw(i):
        for j, (c, r) in enumerate(GROUPS[i]):
            at = i % 2 * 2 + j
            w = w_pair(c, r).astype(F32)
            grad = grads[at][...]
            scale = pl.reciprocal(
                jnp.abs(grad) * (1.0 / INNER_RATE) + ADAM_EPS / INNER_RATE, approx=True
            )
            now = w * (1.0 - INNER_RATE * DECAY_RATE) - grad * scale
            currents[at][...] = now.astype(BF16)

    def columns_forward(i):
        for j, (c, r) in enumerate(GROUPS[i]):
            hold(2 + c, r, dot(h2[...], currents[i % 2 * 2 + j][...]))

    def columns_send(i):
        for c, r in GROUPS[i]:
            send_partial(2 + c, r)

    def stage(i):
        columns_arrive(i)
        if i >= 2:
            columns_forward(i - 2)
        if i >= 1:
            columns_adamw(i - 1)
        columns_gradient(i)
        if i >= 2:
            columns_send(i - 2)

    def last_stages():
        end = len(GROUPS) - 1
        columns_forward(end - 2)
        columns_adamw(end - 1)
        columns_send(end - 2)
        columns_forward(end - 1)
        columns_send(end - 1)
        pass_on(0, FAR)
        pass_on(1, FAR)
        columns_arrive(end)
        columns_gradient(end)
        columns_adamw(end)
        columns_forward(end)
        columns_send(end)

    def fragment_part(k, c, part):
        taken = jnp.where(frag == me, 1.0, 0.0) * tgt[k, :, lanes(c)].astype(F32)
        fpart[k, c] = (part - taken).astype(BF16)

    def fragment_forward():
        for c in range(2):
            fragment_part(0, c, dot(h1[...], w_v[frag * 2 + c]))
        loop(1, NTP, lambda i: f1_copy(0, i).start())

    def fragment_slope(k):
        acc = fpart[k, :, ftoks(me), :].astype(F32)
        for i in range(1, NTP):
            f1_copy(k, i).wait_recv()
            acc = acc + frecv[k, i].astype(F32)
        fslope[k, :, ftoks(me), :] = (acc * (1.0 / tokens)).astype(BF16)
        loop(1, NTP, lambda i: f2_copy(k, i).start())

    def fragment_one():
        loop(1, NTP, lambda i: f2_copy(0, i).wait_recv())
        for c in range(2):
            grad = dot(ht1[...], fslope[0, c])
            anchor = w_v[frag * 2 + c].astype(F32)
            ratio = grad * recip(jnp.abs(grad) + ADAM_EPS)
            after = anchor - INNER_RATE * (ratio + DECAY_RATE * anchor)
            g1f[c] = grad
            synced[c] = after
            drifts[c][...] = (anchor - after).astype(BF16)
            loop(1, NZ, lambda s, c=c: z1_copy(c, s).start())
        for c in range(2):
            fragment_part(1, c, dot(h2[...], synced[c].astype(BF16)))
        loop(1, NTP, lambda i: f1_copy(1, i).start())

    def fragment_two():
        loop(1, NTP, lambda i: f2_copy(1, i).wait_recv())
        for c in range(2):
            grad = dot(ht2[...], fslope[1, c])
            one = g1f[c]
            first = BETA_ONE * (1.0 - BETA_ONE) * one + (1.0 - BETA_ONE) * grad
            second = BETA_TWO * (1.0 - BETA_TWO) * one * one + (1.0 - BETA_TWO) * grad * grad
            ratio = (first * (1.0 / (1.0 - BETA_ONE**2))) / (
                jnp.sqrt(second * (1.0 / (1.0 - BETA_TWO**2))) + ADAM_EPS
            )
            after = synced[c]
            final[c] = after - INNER_RATE * (ratio + DECAY_RATE * after)

    def z_sum(c):
        acc = drifts[c][zpart(rz), :].astype(F32)
        for s in range(1, NZ):
            z1_copy(c, s).wait_recv()
            acc = acc + zrecv[c, s].astype(F32)
        ysend[c] = acc.astype(BF16)
        y_copy(c).start()

    def y_sum(c):
        y_copy(c).wait_recv()
        total[c, zpart(rz), :] = (ysend[c].astype(F32) + yrecv[c].astype(F32)).astype(BF16)
        loop(1, NZ, lambda s: z2_copy(c, s).start())

    def residual_out(c):
        diff = own_sum(2 + c) - tgt[1, :, lanes(c)].astype(F32)
        res_ref[0, lanes(c), :] = diff.T

    def outer(c):
        loop(1, NZ, lambda s: z2_copy(c, s).wait_recv())
        anchor = w_v[frag * 2 + c].astype(F32)
        mean = total[c].astype(F32) * (1.0 / (2 * NZ))
        moved = OUTER_MOMENTUM * mom_v[:, lanes(c)] + mean
        new = anchor - OUTER_RATE * (mean + OUTER_MOMENTUM * moved)
        nm_ref[:, lanes(c)] = moved
        ng_ref[:, lanes(c)] = new
        lf_ref[0, :, lanes(c)] = (MIX_KEEP * final[c] + (1.0 - MIX_KEEP) * new).astype(BF16)

    def sent(u):
        for r in range(NCHIP):
            sib_copy(u, r, r).wait_send()
        for m in range(3):
            rs_copy(u, m).wait_send()

    def hops_sent(u):
        for m in range(3, len(HOPS)):
            rs_copy(u, m).wait_send()

    def slopes_sent(c):
        for m in range(len(SPREAD)):
            ag_copy(c, m).wait_send()
        for r in range(NCHIP):
            agd_copy(c, r).wait_send()

    def fragment_sent(k):
        loop(1, NTP, lambda i: f1_copy(k, i).wait_send())
        loop(1, NTP, lambda i: f2_copy(k, i).wait_send())

    forward_one(0, 0)
    forward_one(0, 1)
    tpool_copy.wait()
    tgt[0] = dot(picks(0), tpool_v[...], 0, 0).astype(BF16)
    forward_one(1, 0)
    hops(0, 2, 1)
    forward_one(1, 1)
    fragment_forward()
    hops(1, 2, 1)
    ht1[...] = dot(pool_v[...], picks(0), 0, 0).astype(BF16)
    hops(0, 3, 4, 5)
    fragment_slope(0)
    hops(1, 3, 4, 5)
    h2[...] = dot(picks(1), pool_v[...], 0, 0).astype(BF16)
    tgt[1] = dot(picks(1), tpool_v[...], 0, 0).astype(BF16)
    hops(0, 6)
    hops(1, 6)
    fragment_one()
    slope_send(0)
    slope_send(1)
    ht2[...] = dot(pool_v[...], picks(1), 0, 0).astype(BF16)
    stage(0)
    pass_on(0, 1, 3, 4)
    pass_on(1, 1, 3, 4)
    fragment_slope(1)
    stage(1)
    stage(2)
    pass_on(0, 5, 7, 2)
    pass_on(1, 5, 7, 2)
    stage(3)
    z_sum(0)
    stage(4)
    stage(5)
    stage(6)
    last_stages()
    y_sum(0)
    hops(2, 2, 1)
    hops(3, 2, 1)
    z_sum(1)
    fragment_two()
    sent(0)
    sent(1)
    hops(2, 3, 4, 5)
    hops(3, 3, 4, 5)
    y_sum(1)
    mom_copy.wait()
    hops_sent(0)
    hops_sent(1)
    hops(2, 6)
    hops(3, 6)
    slopes_sent(0)
    slopes_sent(1)
    fragment_sent(0)
    fragment_sent(1)
    sent(2)
    sent(3)
    outer(0)
    residual_out(0)
    residual_out(1)
    outer(1)

    hops_sent(2)
    hops_sent(3)
    for c in range(2):
        loop(1, NZ, lambda s, c=c: z1_copy(c, s).wait_send())
        y_copy(c).wait_send()
        loop(1, NZ, lambda s, c=c: z2_copy(c, s).wait_send())


def copy_out(*refs):
    sem = refs[-1]
    copies = [pltpu.make_async_copy(refs[i], refs[4 + i], sem.at[i]) for i in range(4)]
    for copy in copies:
        copy.start()
    for copy in copies:
        copy.wait()


def body(weights, hidden_pool, target_pool, token_rows, fragment, outer_momentum):
    depth, features = weights.shape
    pool = hidden_pool.shape[1]
    width = outer_momentum.shape[1]
    owned = target_pool.shape[2]
    tokens = token_rows.shape[2]
    zrows = depth // NZ
    blocks = features // LANES
    dma = pltpu.SemaphoreType.DMA
    scratch = [
        pltpu.VMEM((blocks, depth, LANES), BF16),
        pltpu.VMEM((pool, depth), BF16),
        pltpu.VMEM((pool, owned), BF16),
        pltpu.VMEM((depth, width), F32),
        pltpu.VMEM((tokens, depth), BF16),
        pltpu.VMEM((tokens, depth), BF16),
        pltpu.VMEM((depth, tokens), BF16),
        pltpu.VMEM((depth, tokens), BF16),
        pltpu.VMEM((2, tokens, owned), BF16),
        *[pltpu.VMEM((4, NCHIP, tokens, LANES), BF16)] * 5,
        *[pltpu.VMEM((NTP, tokens, LANES), BF16)] * 2,
        *[pltpu.VMEM((depth, 2 * LANES), F32)] * 4,
        *[pltpu.VMEM((depth, 2 * LANES), BF16)] * 4,
        pltpu.VMEM((2, depth, LANES), F32),
        pltpu.VMEM((2, depth, LANES), F32),
        *[pltpu.VMEM((depth, LANES), BF16)] * 2,
        pltpu.VMEM((2, 2, tokens, LANES), BF16),
        pltpu.VMEM((2, NTP, 2, tokens // NTP, LANES), BF16),
        pltpu.VMEM((2, 2, tokens, LANES), BF16),
        pltpu.VMEM((2, depth, LANES), F32),
        pltpu.VMEM((2, NZ, zrows, LANES), BF16),
        pltpu.VMEM((2, zrows, LANES), BF16),
        pltpu.VMEM((2, zrows, LANES), BF16),
        pltpu.VMEM((2, depth, LANES), BF16),
        dma((2, NCHIP, 2)),
        dma((3,)),
        *[dma((4, NCHIP))] * 4,
        *[dma((2, NCHIP))] * 4,
        *[dma((2, NTP))] * 4,
        dma((2, NZ)),
        dma((2, NZ)),
        dma((2,)),
        dma((2,)),
        dma((2, NZ)),
        dma((2, NZ)),
    ]
    hbm = pl.BlockSpec(memory_space=pl.ANY)
    vmem = pl.BlockSpec(memory_space=pltpu.VMEM)
    smem = pl.BlockSpec(memory_space=pltpu.SMEM)
    results = (
        jax.ShapeDtypeStruct((depth, width), F32),
        jax.ShapeDtypeStruct((depth, width), F32),
        jax.ShapeDtypeStruct((1, depth, width), BF16),
        jax.ShapeDtypeStruct((1, owned, tokens), F32),
    )
    held = pl.pallas_call(
        kernel,
        out_shape=tuple(pltpu.VMEM(r.shape, r.dtype) for r in results),
        in_specs=[hbm, hbm, hbm, vmem, smem, hbm],
        out_specs=(vmem, vmem, vmem, vmem),
        scratch_shapes=scratch,
        compiler_params=pltpu.CompilerParams(
            collective_id=0, has_side_effects=True, vmem_limit_bytes=56 * 1024 * 1024
        ),
    )(weights, hidden_pool, target_pool, token_rows[0], fragment, outer_momentum)
    return pl.pallas_call(
        copy_out,
        out_shape=results,
        in_specs=[hbm] * 4,
        out_specs=(hbm,) * 4,
        scratch_shapes=[dma((4,))],
        compiler_params=pltpu.CompilerParams(vmem_limit_bytes=4 * 1024 * 1024),
    )(*held)


def solution(mesh):
    in_specs = (
        P("tp", None),
        P("rep", None, "tp"),
        P("rep", None, "tp"),
        P("rep", None, None),
        P(),
        P("tp", None),
    )
    out_specs = (P("tp", None), P("tp", None), P("rep", "tp", None), P("rep", "tp", None))
    return jax.shard_map(body, mesh=mesh, in_specs=in_specs, out_specs=out_specs, check_vma=False)
```

```python
import functools

import jax
import jax.numpy as jnp
from jax import lax
from jax.experimental import pallas as pl
from jax.experimental.pallas import tpu as pltpu
from jax.sharding import PartitionSpec as P

BETA_ONE = 0.9
BETA_TWO = 0.95
INNER_RATE = 0.001
DECAY_RATE = 0.1
ADAM_EPS = 0.001
OUTER_RATE = 0.7
OUTER_MOMENTUM = 0.9
MIX_KEEP = 0.5

MESH = pl.DeviceIdType.MESH
F32 = jnp.float32
BF16 = jnp.bfloat16

NX = 4
NCHIP = 8
NTP = 16
NZ = 8
LANES = 128


def dot(a, b, ca=1, cb=0):
    return lax.dot_general(a, b, (((ca,), (cb,)), ((), ())), preferred_element_type=F32)


def recip(x):
    r = pl.reciprocal(x, approx=True)
    return r * (2.0 - x * r)


AHEAD, BEHIND, ACROSS = 1, NX - 1, NX
HOPS = (
    (6, None, AHEAD),
    (7, None, BEHIND),
    (2, None, BEHIND),
    (5, 0, ACROSS),
    (4, 1, ACROSS),
    (3, 2, BEHIND),
    (1, 3, AHEAD),
)
LAST_HOPS = (4, 5, 6)
SPREAD = (
    (0, AHEAD, 3),
    (0, BEHIND, 1),
    (0, ACROSS, 4),
    (1, ACROSS, 5),
    (4, AHEAD, 7),
    (3, AHEAD, 2),
    (5, BEHIND, 6),
)
OUTWARD = (6, 2, 7, 5, 4, 3, 1, 0)
FAR = 6
GROUPS = (
    ((0, 0), (1, 0)),
    ((0, 1), (0, 3)),
    ((0, 4), (1, 1)),
    ((1, 3), (1, 4)),
    ((0, 5), (0, 7)),
    ((0, 2), (1, 5)),
    ((1, 7), (1, 2)),
    ((0, 6), (1, 6)),
)


def mirror(r):
    return r // NX * NX + (NX - r % NX) % NX


def kernel(
    w_hbm, pool_hbm, tpool_hbm, rows_ref, frag_ref, mom_hbm,
    nm_ref, ng_ref, lf_ref, res_ref,
    w_v, pool_v, tpool_v, mom_v,
    h1, h2, ht1, ht2, tgt,
    keep, sibs, sibr, rss, rsr,
    slope0, slope1, grad0, grad1, grad2, grad3, cur0, cur1, cur2, cur3,
    g1f, synced, drift0, drift1, fpart, frecv, fslope, final,
    zrecv, ysend, yrecv, total,
    w_sem, in_sem,
    sib_s, sib_r, rs_s, rs_r, ag_s, ag_r, agd_s, agd_r,
    f1_s, f1_r, f2_s, f2_r, z1_s, z1_r, y_s, y_r, z2_s, z2_r,
):
    tokens = rows_ref.shape[1]
    pool = pool_v.shape[0]
    depth = w_v.shape[1]
    zrows = depth // NZ
    ftok = tokens // NTP

    me = lax.axis_index("tp")
    core = lax.rem(me, 2)
    chip = lax.div(me, 2)
    cy = lax.div(chip, NX)
    cx = lax.rem(chip, NX)
    rep = lax.axis_index("rep")
    rz = lax.div(rep, 2)
    ry = lax.rem(rep, 2)
    sibling = chip * 2 + 1 - core
    frag = frag_ref[0]
    slopes = (slope0, slope1)
    drifts = (drift0, drift1)
    grads = (grad0, grad1, grad2, grad3)
    currents = (cur0, cur1, cur2, cur3)

    def chip_at(r):
        return lax.rem(cy + r // NX, 2) * NX + lax.rem(cx + r % NX * (1 + 2 * core), NX)

    def rep_at(s):
        return lax.rem(rz + s, NZ) * 2 + ry

    def loop(lo, hi, body):
        def step(i, carry):
            body(i)
            return carry

        lax.fori_loop(lo, hi, step, 0)

    def w_copy(c, r, j):
        slot = (chip_at(r) * 2 + j) * 2 + c
        return pltpu.make_async_copy(
            w_hbm.at[:, pl.ds(pl.multiple_of(slot * LANES, LANES), LANES)],
            w_v.at[slot],
            w_sem.at[c, r, j],
        )

    pool_copy = pltpu.make_async_copy(pool_hbm.at[0], pool_v, in_sem.at[0])
    tpool_copy = pltpu.make_async_copy(tpool_hbm.at[0], tpool_v, in_sem.at[1])
    mom_copy = pltpu.make_async_copy(mom_hbm, mom_v, in_sem.at[2])
    pool_copy.start()
    for c in range(2):
        for r in OUTWARD:
            w_copy(c, r, 0).start()
            w_copy(c, r, 1).start()
    tpool_copy.start()
    mom_copy.start()

    barrier = pltpu.get_barrier_semaphore()

    def greet_tp(i):
        pl.semaphore_signal(
            barrier, inc=1, device_id={"tp": lax.rem(me + i, NTP)}, device_id_type=MESH
        )

    def greet_z(i):
        pl.semaphore_signal(barrier, inc=1, device_id={"rep": rep_at(i)}, device_id_type=MESH)

    loop(1, NTP, greet_tp)
    loop(1, NZ, greet_z)
    pl.semaphore_signal(barrier, inc=1, device_id={"rep": rz * 2 + 1 - ry}, device_id_type=MESH)

    def picks(k):
        at = lax.broadcasted_iota(jnp.int32, (pool, tokens), 0)
        return jnp.where(at == rows_ref[pl.ds(k, 1), :], 1.0, 0.0).astype(BF16)

    pool_copy.wait()
    h1[...] = dot(picks(0), pool_v[...], 0, 0).astype(BF16)

    def sib_copy(u, r, to):
        return pltpu.make_async_remote_copy(
            src_ref=sibs.at[u, r], dst_ref=sibr.at[u, to],
            send_sem=sib_s.at[u, r], recv_sem=sib_r.at[u, to],
            device_id={"tp": sibling}, device_id_type=MESH,
        )

    def far_copy(u):
        return pltpu.make_async_remote_copy(
            src_ref=sibs.at[u, FAR], dst_ref=sibr.at[u, FAR],
            send_sem=sib_s.at[u, FAR], recv_sem=sib_r.at[u, FAR],
            device_id={"tp": chip_at(BEHIND) * 2 + 1 - core}, device_id_type=MESH,
        )

    def rs_copy(u, m):
        return pltpu.make_async_remote_copy(
            src_ref=keep.at[u, FAR] if m == 0 else rss.at[u, m], dst_ref=rsr.at[u, m],
            send_sem=rs_s.at[u, m], recv_sem=rs_r.at[u, m],
            device_id={"tp": chip_at(HOPS[m][2]) * 2 + core}, device_id_type=MESH,
        )

    def ag_copy(c, m):
        here, to, there = SPREAD[m]
        owner = chip_at(here) * 2 + core
        return pltpu.make_async_remote_copy(
            src_ref=slopes[c].at[owner], dst_ref=slopes[c].at[owner],
            send_sem=ag_s.at[c, m], recv_sem=ag_r.at[c, there],
            device_id={"tp": chip_at(to) * 2 + core}, device_id_type=MESH,
        )

    def ag_arrival(c, r):
        owner = chip_at(r) * 2 + core
        return pltpu.make_async_remote_copy(
            src_ref=slopes[c].at[owner], dst_ref=slopes[c].at[owner],
            send_sem=ag_s.at[c, 0], recv_sem=ag_r.at[c, r],
            device_id={"tp": sibling}, device_id_type=MESH,
        )

    def agd_copy(c, r):
        owner = chip_at(r) * 2 + core
        return pltpu.make_async_remote_copy(
            src_ref=slopes[c].at[owner], dst_ref=slopes[c].at[owner],
            send_sem=agd_s.at[c, r], recv_sem=agd_r.at[c, mirror(r)],
            device_id={"tp": sibling}, device_id_type=MESH,
        )

    def ag_far(c):
        owner = chip_at(5) * 2 + core
        return pltpu.make_async_remote_copy(
            src_ref=slopes[c].at[owner], dst_ref=slopes[c].at[owner],
            send_sem=agd_s.at[c, FAR], recv_sem=agd_r.at[c, FAR],
            device_id={"tp": chip_at(BEHIND) * 2 + 1 - core}, device_id_type=MESH,
        )

    def agd_arrival(c, r):
        owner = chip_at(r) * 2 + 1 - core
        return pltpu.make_async_remote_copy(
            src_ref=slopes[c].at[owner], dst_ref=slopes[c].at[owner],
            send_sem=agd_s.at[c, r], recv_sem=agd_r.at[c, r],
            device_id={"tp": sibling}, device_id_type=MESH,
        )

    def ftoks(i):
        return pl.ds(pl.multiple_of(i * ftok, ftok), ftok)

    def f1_copy(k, i):
        to = lax.rem(me + i, NTP)
        return pltpu.make_async_remote_copy(
            src_ref=fpart.at[k, :, ftoks(to), :], dst_ref=frecv.at[k, i],
            send_sem=f1_s.at[k, i], recv_sem=f1_r.at[k, i],
            device_id={"tp": to}, device_id_type=MESH,
        )

    def f2_copy(k, i):
        to = lax.rem(me + i, NTP)
        return pltpu.make_async_remote_copy(
            src_ref=fslope.at[k, :, ftoks(me), :], dst_ref=fslope.at[k, :, ftoks(me), :],
            send_sem=f2_s.at[k, i], recv_sem=f2_r.at[k, i],
            device_id={"tp": to}, device_id_type=MESH,
        )

    def zpart(i):
        return pl.ds(pl.multiple_of(i * zrows, 16), zrows)

    def z1_copy(c, s):
        return pltpu.make_async_remote_copy(
            src_ref=drifts[c].at[zpart(lax.rem(rz + s, NZ)), :], dst_ref=zrecv.at[c, s],
            send_sem=z1_s.at[c, s], recv_sem=z1_r.at[c, s],
            device_id={"rep": rep_at(s)}, device_id_type=MESH,
        )

    def y_copy(c):
        return pltpu.make_async_remote_copy(
            src_ref=ysend.at[c], dst_ref=yrecv.at[c],
            send_sem=y_s.at[c], recv_sem=y_r.at[c],
            device_id={"rep": rz * 2 + 1 - ry}, device_id_type=MESH,
        )

    def z2_copy(c, s):
        return pltpu.make_async_remote_copy(
            src_ref=total.at[c, zpart(rz), :], dst_ref=total.at[c, zpart(rz), :],
            send_sem=z2_s.at[c, s], recv_sem=z2_r.at[c, s],
            device_id={"rep": rep_at(s)}, device_id_type=MESH,
        )

    def lanes(c):
        return pl.ds(c * LANES, LANES)

    def w_pair(c, r):
        q = chip_at(r)
        mine = w_v[(q * 2 + core) * 2 + c]
        other = w_v[(q * 2 + 1 - core) * 2 + c]
        return jnp.concatenate([mine, other], axis=1)

    def hold(u, r, part):
        keep[u, r] = part[:, :LANES].astype(BF16)
        sibs[u, r] = part[:, LANES:].astype(BF16)

    def both(u, r):
        sib_copy(u, r, r).wait_recv()
        return keep[u, r].astype(F32) + sibr[u, r].astype(F32)

    def send_partial(u, r):
        if r == FAR:
            rs_copy(u, 0).start()
            far_copy(u).start()
        else:
            sib_copy(u, r, mirror(r)).start()

    def hop(u, m):
        r, added, _ = HOPS[m]
        acc = both(u, r)
        if added == 0:
            far_copy(u).wait_recv()
            acc = acc + sibr[u, FAR].astype(F32)
        if added is not None:
            rs_copy(u, added).wait_recv()
            acc = acc + rsr[u, added].astype(F32)
        rss[u, m] = acc.astype(BF16)
        rs_copy(u, m).start()

    def hops(u, *messages):
        for m in messages:
            hop(u, m)

    def own_sum(u):
        acc = both(u, 0)
        for m in LAST_HOPS:
            rs_copy(u, m).wait_recv()
            acc = acc + rsr[u, m].astype(F32)
        return acc

    def w_arrive(c, half):
        for r in OUTWARD[half * 4 : half * 4 + 4]:
            w_copy(c, r, 0).wait()
            w_copy(c, r, 1).wait()

    def forward_one(c, half):
        group = OUTWARD[half * 4 : half * 4 + 4]
        if (c, half) != (1, 1):
            w_arrive(c, half)
        for r in group:
            hold(c, r, dot(h1[...], w_pair(c, r)))
        if c == 0 and half == 0:
            pl.semaphore_wait(barrier, NTP - 1 + NZ)
        for r in group:
            send_partial(c, r)

    def slope_send(c):
        diff = own_sum(c) - tgt[0, :, lanes(c)].astype(F32)
        slopes[c][me] = (diff * (1.0 / tokens)).astype(BF16)
        for m in range(3):
            ag_copy(c, m).start()
        agd_copy(c, 0).start()

    def pass_on(c, *places):
        for r in places:
            ag_arrival(c, r).wait_recv()
            for m in range(3, len(SPREAD)):
                if SPREAD[m][0] == r:
                    ag_copy(c, m).start()
            if r == 5:
                ag_far(c).start()
            if r != FAR:
                agd_copy(c, r).start()

    def columns_arrive(i):
        for c, r in GROUPS[i]:
            agd_arrival(c, r).wait_recv()

    def columns_gradient(i):
        for j, (c, r) in enumerate(GROUPS[i]):
            q = chip_at(r)
            mine, other = slopes[c][q * 2 + core], slopes[c][q * 2 + 1 - core]
            grads[i % 2 * 2 + j][...] = dot(ht1[...], jnp.concatenate([mine, other], axis=1))

    def columns_adamw(i):
        for j, (c, r) in enumerate(GROUPS[i]):
            at = i % 2 * 2 + j
            w = w_pair(c, r).astype(F32)
            grad = grads[at][...]
            scale = pl.reciprocal(
                jnp.abs(grad) * (1.0 / INNER_RATE) + ADAM_EPS / INNER_RATE, approx=True
            )
            now = w * (1.0 - INNER_RATE * DECAY_RATE) - grad * scale
            currents[at][...] = now.astype(BF16)

    def columns_forward(i):
        for j, (c, r) in enumerate(GROUPS[i]):
            hold(2 + c, r, dot(h2[...], currents[i % 2 * 2 + j][...]))

    def columns_send(i):
        for c, r in GROUPS[i]:
            send_partial(2 + c, r)

    def stage(i):
        columns_arrive(i)
        if i >= 2:
            columns_forward(i - 2)
        if i >= 1:
            columns_adamw(i - 1)
        columns_gradient(i)
        if i >= 2:
            columns_send(i - 2)

    def last_stages():
        end = len(GROUPS) - 1
        columns_forward(end - 2)
        columns_adamw(end - 1)
        columns_send(end - 2)
        columns_forward(end - 1)
        columns_send(end - 1)
        pass_on(0, FAR)
        pass_on(1, FAR)
        columns_arrive(end)
        columns_gradient(end)
        columns_adamw(end)
        columns_forward(end)
        columns_send(end)

    def fragment_part(k, c, part):
        taken = jnp.where(frag == me, 1.0, 0.0) * tgt[k, :, lanes(c)].astype(F32)
        fpart[k, c] = (part - taken).astype(BF16)

    def fragment_forward():
        for c in range(2):
            fragment_part(0, c, dot(h1[...], w_v[frag * 2 + c]))
        loop(1, NTP, lambda i: f1_copy(0, i).start())

    def fragment_slope(k):
        acc = fpart[k, :, ftoks(me), :].astype(F32)
        for i in range(1, NTP):
            f1_copy(k, i).wait_recv()
            acc = acc + frecv[k, i].astype(F32)
        fslope[k, :, ftoks(me), :] = (acc * (1.0 / tokens)).astype(BF16)
        loop(1, NTP, lambda i: f2_copy(k, i).start())

    def fragment_one():
        loop(1, NTP, lambda i: f2_copy(0, i).wait_recv())
        for c in range(2):
            grad = dot(ht1[...], fslope[0, c])
            anchor = w_v[frag * 2 + c].astype(F32)
            ratio = grad * recip(jnp.abs(grad) + ADAM_EPS)
            after = anchor - INNER_RATE * (ratio + DECAY_RATE * anchor)
            g1f[c] = grad
            synced[c] = after
            drifts[c][...] = (anchor - after).astype(BF16)
            loop(1, NZ, lambda s, c=c: z1_copy(c, s).start())
        for c in range(2):
            fragment_part(1, c, dot(h2[...], synced[c].astype(BF16)))
        loop(1, NTP, lambda i: f1_copy(1, i).start())

    def fragment_two():
        loop(1, NTP, lambda i: f2_copy(1, i).wait_recv())
        for c in range(2):
            grad = dot(ht2[...], fslope[1, c])
            one = g1f[c]
            first = BETA_ONE * (1.0 - BETA_ONE) * one + (1.0 - BETA_ONE) * grad
            second = BETA_TWO * (1.0 - BETA_TWO) * one * one + (1.0 - BETA_TWO) * grad * grad
            ratio = (first * (1.0 / (1.0 - BETA_ONE**2))) / (
                jnp.sqrt(second * (1.0 / (1.0 - BETA_TWO**2))) + ADAM_EPS
            )
            after = synced[c]
            final[c] = after - INNER_RATE * (ratio + DECAY_RATE * after)

    def z_sum(c):
        acc = drifts[c][zpart(rz), :].astype(F32)
        for s in range(1, NZ):
            z1_copy(c, s).wait_recv()
            acc = acc + zrecv[c, s].astype(F32)
        ysend[c] = acc.astype(BF16)
        y_copy(c).start()

    def y_sum(c):
        y_copy(c).wait_recv()
        total[c, zpart(rz), :] = (ysend[c].astype(F32) + yrecv[c].astype(F32)).astype(BF16)
        loop(1, NZ, lambda s: z2_copy(c, s).start())

    def residual_out(c):
        diff = own_sum(2 + c) - tgt[1, :, lanes(c)].astype(F32)
        res_ref[0, lanes(c), :] = diff.T

    def outer(c):
        loop(1, NZ, lambda s: z2_copy(c, s).wait_recv())
        anchor = w_v[frag * 2 + c].astype(F32)
        mean = total[c].astype(F32) * (1.0 / (2 * NZ))
        moved = OUTER_MOMENTUM * mom_v[:, lanes(c)] + mean
        new = anchor - OUTER_RATE * (mean + OUTER_MOMENTUM * moved)
        nm_ref[:, lanes(c)] = moved
        ng_ref[:, lanes(c)] = new
        lf_ref[0, :, lanes(c)] = (MIX_KEEP * final[c] + (1.0 - MIX_KEEP) * new).astype(BF16)

    def sent(u):
        for r in range(NCHIP):
            sib_copy(u, r, r).wait_send()
        for m in range(3):
            rs_copy(u, m).wait_send()

    def hops_sent(u):
        for m in range(3, len(HOPS)):
            rs_copy(u, m).wait_send()

    def slopes_sent(c):
        for m in range(len(SPREAD)):
            ag_copy(c, m).wait_send()
        for r in range(NCHIP):
            agd_copy(c, r).wait_send()

    def fragment_sent(k):
        loop(1, NTP, lambda i: f1_copy(k, i).wait_send())
        loop(1, NTP, lambda i: f2_copy(k, i).wait_send())

    forward_one(0, 0)
    forward_one(0, 1)
    tpool_copy.wait()
    tgt[0] = dot(picks(0), tpool_v[...], 0, 0).astype(BF16)
    forward_one(1, 0)
    w_arrive(1, 1)
    fragment_forward()
    hops(0, 2, 1)
    forward_one(1, 1)
    hops(1, 2, 1)
    ht1[...] = dot(pool_v[...], picks(0), 0, 0).astype(BF16)
    hops(0, 3, 4, 5)
    fragment_slope(0)
    hops(1, 3, 4, 5)
    h2[...] = dot(picks(1), pool_v[...], 0, 0).astype(BF16)
    tgt[1] = dot(picks(1), tpool_v[...], 0, 0).astype(BF16)
    hops(0, 6)
    hops(1, 6)
    fragment_one()
    slope_send(0)
    slope_send(1)
    ht2[...] = dot(pool_v[...], picks(1), 0, 0).astype(BF16)
    stage(0)
    pass_on(0, 1, 3, 4)
    pass_on(1, 1, 3, 4)
    fragment_slope(1)
    stage(1)
    stage(2)
    pass_on(0, 5, 7, 2)
    pass_on(1, 5, 7, 2)
    stage(3)
    z_sum(0)
    stage(4)
    stage(5)
    stage(6)
    last_stages()
    y_sum(0)
    hops(2, 2, 1)
    hops(3, 2, 1)
    z_sum(1)
    fragment_two()
    sent(0)
    sent(1)
    hops(2, 3, 4, 5)
    hops(3, 3, 4, 5)
    y_sum(1)
    mom_copy.wait()
    hops_sent(0)
    hops_sent(1)
    hops(2, 6)
    hops(3, 6)
    slopes_sent(0)
    slopes_sent(1)
    fragment_sent(0)
    fragment_sent(1)
    sent(2)
    sent(3)
    outer(0)
    residual_out(0)
    residual_out(1)
    outer(1)

    hops_sent(2)
    hops_sent(3)
    for c in range(2):
        loop(1, NZ, lambda s, c=c: z1_copy(c, s).wait_send())
        y_copy(c).wait_send()
        loop(1, NZ, lambda s, c=c: z2_copy(c, s).wait_send())


def copy_out(*refs):
    sem = refs[-1]
    copies = [pltpu.make_async_copy(refs[i], refs[4 + i], sem.at[i]) for i in range(4)]
    for copy in copies:
        copy.start()
    for copy in copies:
        copy.wait()


def body(weights, hidden_pool, target_pool, token_rows, fragment, outer_momentum):
    depth, features = weights.shape
    pool = hidden_pool.shape[1]
    width = outer_momentum.shape[1]
    owned = target_pool.shape[2]
    tokens = token_rows.shape[2]
    zrows = depth // NZ
    blocks = features // LANES
    dma = pltpu.SemaphoreType.DMA
    scratch = [
        pltpu.VMEM((blocks, depth, LANES), BF16),
        pltpu.VMEM((pool, depth), BF16),
        pltpu.VMEM((pool, owned), BF16),
        pltpu.VMEM((depth, width), F32),
        pltpu.VMEM((tokens, depth), BF16),
        pltpu.VMEM((tokens, depth), BF16),
        pltpu.VMEM((depth, tokens), BF16),
        pltpu.VMEM((depth, tokens), BF16),
        pltpu.VMEM((2, tokens, owned), BF16),
        *[pltpu.VMEM((4, NCHIP, tokens, LANES), BF16)] * 5,
        *[pltpu.VMEM((NTP, tokens, LANES), BF16)] * 2,
        *[pltpu.VMEM((depth, 2 * LANES), F32)] * 4,
        *[pltpu.VMEM((depth, 2 * LANES), BF16)] * 4,
        pltpu.VMEM((2, depth, LANES), F32),
        pltpu.VMEM((2, depth, LANES), F32),
        *[pltpu.VMEM((depth, LANES), BF16)] * 2,
        pltpu.VMEM((2, 2, tokens, LANES), BF16),
        pltpu.VMEM((2, NTP, 2, tokens // NTP, LANES), BF16),
        pltpu.VMEM((2, 2, tokens, LANES), BF16),
        pltpu.VMEM((2, depth, LANES), F32),
        pltpu.VMEM((2, NZ, zrows, LANES), BF16),
        pltpu.VMEM((2, zrows, LANES), BF16),
        pltpu.VMEM((2, zrows, LANES), BF16),
        pltpu.VMEM((2, depth, LANES), BF16),
        dma((2, NCHIP, 2)),
        dma((3,)),
        *[dma((4, NCHIP))] * 4,
        *[dma((2, NCHIP))] * 4,
        *[dma((2, NTP))] * 4,
        dma((2, NZ)),
        dma((2, NZ)),
        dma((2,)),
        dma((2,)),
        dma((2, NZ)),
        dma((2, NZ)),
    ]
    hbm = pl.BlockSpec(memory_space=pl.ANY)
    vmem = pl.BlockSpec(memory_space=pltpu.VMEM)
    smem = pl.BlockSpec(memory_space=pltpu.SMEM)
    results = (
        jax.ShapeDtypeStruct((depth, width), F32),
        jax.ShapeDtypeStruct((depth, width), F32),
        jax.ShapeDtypeStruct((1, depth, width), BF16),
        jax.ShapeDtypeStruct((1, owned, tokens), F32),
    )
    held = pl.pallas_call(
        kernel,
        out_shape=tuple(pltpu.VMEM(r.shape, r.dtype) for r in results),
        in_specs=[hbm, hbm, hbm, vmem, smem, hbm],
        out_specs=(vmem, vmem, vmem, vmem),
        scratch_shapes=scratch,
        compiler_params=pltpu.CompilerParams(
            collective_id=0, has_side_effects=True, vmem_limit_bytes=56 * 1024 * 1024
        ),
    )(weights, hidden_pool, target_pool, token_rows[0], fragment, outer_momentum)
    return pl.pallas_call(
        copy_out,
        out_shape=results,
        in_specs=[hbm] * 4,
        out_specs=(hbm,) * 4,
        scratch_shapes=[dma((4,))],
        compiler_params=pltpu.CompilerParams(vmem_limit_bytes=4 * 1024 * 1024),
    )(*held)


def solution(mesh):
    in_specs = (
        P("tp", None),
        P("rep", None, "tp"),
        P("rep", None, "tp"),
        P("rep", None, None),
        P(),
        P("tp", None),
    )
    out_specs = (P("tp", None), P("tp", None), P("rep", "tp", None), P("rep", "tp", None))
    return jax.shard_map(body, mesh=mesh, in_specs=in_specs, out_specs=out_specs, check_vma=False)
```
